256 devices in a mesh: dp: 16 (over y_lo, z), tensor: 16 (over x, y_hi, core).
Axes of the slice: x: 4, y: 4 (y_hi: 2, y_lo: 2; y = y_hi * 2 + y_lo), z: 8, core: 2. Of those that a mesh axis runs over, the one named last changes fastest.
Arguments:
- tokens: bfloat16 [4096, 5120], P('dp', 'tensor'), may hold values from -6 to 6
- upstream: bfloat16 [4096, 5120], P('dp', 'tensor'), may hold values from -6 to 6
- gate_weight: bfloat16 [5120, 8192], P('dp', 'tensor'), may hold values from -0.078125 to 0.078125
- up_weight: bfloat16 [5120, 8192], P('dp', 'tensor'), may hold values from -0.078125 to 0.078125
- down_weight: bfloat16 [5120, 8192], P('dp', 'tensor'), may hold values from -0.0625 to 0.0625
- adapter_a: bfloat16 [5120, 128], replicated, may hold values from -0.078125 to 0.078125
- adapter_b: bfloat16 [128, 8192], P(None, 'tensor'), may hold values from -0.75 to 0.75
- membership: int32 [4096], P('dp'), may hold values from 0 to 255, as said below
Outputs:
- log_ratio: float32 [4096], P('dp')
- input_grad: bfloat16 [4096, 5120], P('dp', 'tensor')
- adapter_b_gradient: float32 [128, 8192], P('dp', 'tensor')
The draws below stay inside these ranges and needn't reach their ends.
Inputs may be any that keep to these rules, and one draw needn't show every extreme that they name: `membership`: each aligned block of 256 rows holds every number 0 to 255 once.
All inputs are finite; a program needn't handle non-finite values.
Results may differ from the reference program's by a relative error of at most 0.022.
Values may be sent and summed in bfloat16 or wider, within the bound.
A program may use at most 128 MiB of HBM per device.

```python
import math
import jax
import jax.numpy as jnp
from jax import lax

D = 5120
FF = 8192
R = 64
TOK_DEV = 256
TOKENS = 4096


def draw_membership(key, part):
    key = jax.random.fold_in(key, 7)
    keys = jax.random.split(key, TOKENS // TOK_DEV)

    def one_block(block_key):
        return jax.random.permutation(block_key, TOK_DEV)
    return jax.vmap(one_block)(keys).reshape(-1).astype(jnp.int32)


def steps_of(stream_key, shape, shards, least, largest):
    loudness = 1.0
    for axis_at, shards_of in shards:
        heights = jax.random.uniform(jax.random.fold_in(jax.random.fold_in(stream_key, 6), axis_at), (shards_of,), jnp.float32, least / len(shards), largest / len(shards))
        loudness = loudness * jnp.repeat(jnp.exp(heights), shape[axis_at] // shards_of).reshape((-1,) + (1,) * (len(shape) - 1 - axis_at))
    return loudness


def centred(key, dims, deviation, bound, shards=(), kind=jnp.bfloat16):
    array = deviation * jax.random.normal(key, dims, jnp.float32)
    if shards:
        array = array * steps_of(key, dims, shards, -0.22, 0.18)
    return jnp.clip(array, -bound, bound).astype(kind)


def setup_inputs(seed: int = 0) -> dict:
    key_of = jax.random.split(jax.random.key(seed), 9)
    return {
        "tokens": centred(key_of[0], (TOKENS, D), 1.0, 6.0, ((0, 16), (1, 16))),
        "upstream": centred(key_of[1], (TOKENS, D), 1.0, 6.0, ((0, 16), (1, 16))),
        "gate_weight": centred(key_of[2], (D, FF), D ** -0.5, 0.078125, ((0, 16), (1, 16))),
        "up_weight": centred(key_of[3], (D, FF), D ** -0.5, 0.078125, ((0, 16), (1, 16))),
        "down_weight": centred(key_of[4], (D, FF), FF ** -0.5, 0.0625, ((0, 16), (1, 16))),
        "adapter_a": centred(key_of[5], (D, 2 * R), D ** -0.5, 0.078125),
        "adapter_b": centred(key_of[6], (2 * R, FF), R ** -0.5, 0.75, ((1, 16),)),
        "membership": draw_membership(jax.random.fold_in(key_of[8], 71), 0),
    }


adapter_scale = 0.5
beta_coef = 0.5
loss_scale = 128.0

def transposed_product(left, right):
    return lax.dot_general(left, right, (((1,), (1,)), ((), ())), preferred_element_type=jnp.float32)

def lowrank_product(left, right):
    return lax.dot_general(left, right, (((0,), (0,)), ((), ())), preferred_element_type=jnp.float32)

def reference(tokens, upstream, gate_weight, up_weight, down_weight, adapter_a, adapter_b, membership):
    gate_activation = jnp.dot(tokens, gate_weight, preferred_element_type=jnp.float32)
    up_activation = jnp.dot(tokens, up_weight, preferred_element_type=jnp.float32)
    readout = jnp.dot(upstream, down_weight, preferred_element_type=jnp.float32)
    low = jnp.dot(tokens, adapter_a, preferred_element_type=jnp.float32).astype(jnp.bfloat16)
    gate_lowrank = low[:, :R]
    up_lowrank = low[:, R:]
    gate_adapter_right = adapter_b[:R]
    up_adapter_right = adapter_b[R:]
    policy_gate = gate_activation + adapter_scale * jnp.dot(gate_lowrank, gate_adapter_right, preferred_element_type=jnp.float32)
    policy_up = up_activation + adapter_scale * jnp.dot(up_lowrank, up_adapter_right, preferred_element_type=jnp.float32)
    shift = jax.nn.silu(policy_gate) * policy_up - jax.nn.silu(gate_activation) * up_activation
    log_ratio = lax.optimization_barrier(jnp.sum(shift * readout, axis=1)) / math.sqrt(D)
    rows = jnp.arange(TOKENS, dtype=jnp.int32)
    pair_id = rows // TOK_DEV * (TOK_DEV // 2) + membership // 2
    side = (1 - 2 * (membership % 2)).astype(jnp.float32)
    link = jnp.exp(log_ratio) + log_ratio
    margin = beta_coef * jax.ops.segment_sum(side * link, pair_id, num_segments=TOKENS // 2)
    pair_weight = -loss_scale * beta_coef * jax.nn.sigmoid(-margin)
    coeff = pair_weight[pair_id] * side * (jnp.exp(log_ratio) + 1.0)
    d_hidden = coeff[:, None] * readout / math.sqrt(D)
    sig = jax.nn.sigmoid(policy_gate)
    dsilu = sig * (1.0 + policy_gate * (1.0 - sig))
    gate_gradient = (d_hidden * policy_up * dsilu).astype(jnp.bfloat16)
    up_gradient = (d_hidden * policy_gate * sig).astype(jnp.bfloat16)
    lowrank_gradient = (adapter_scale * jnp.concatenate([transposed_product(gate_gradient, gate_adapter_right), transposed_product(up_gradient, up_adapter_right)], axis=1)).astype(jnp.bfloat16)
    grad_sum = transposed_product(gate_gradient, gate_weight) + transposed_product(up_gradient, up_weight) + transposed_product(lowrank_gradient, adapter_a)
    input_grad = grad_sum.astype(jnp.bfloat16)
    adapter_b_gradient = adapter_scale * jnp.concatenate([lowrank_product(gate_lowrank, gate_gradient), lowrank_product(up_lowrank, up_gradient)], axis=0)
    return (log_ratio, input_grad, adapter_b_gradient)
```

```python
import math

import jax
import jax.numpy as jnp
from jax import lax
from jax.experimental import pallas as pl
from jax.experimental.pallas import tpu as pltpu
from jax.sharding import PartitionSpec as P

MESH = pl.DeviceIdType.MESH
BF16 = jnp.bfloat16
F32 = jnp.float32

adapter_scale = 0.5
beta_coef = 0.5
loss_scale = 128.0

ROWS = 256
BLK = 320
COLS = 256
RANK = 64
D = 5120


def nt(left, right):
    return lax.dot_general(left, right, (((1,), (1,)), ((), ())), preferred_element_type=F32)


def dot(left, right):
    return jnp.dot(left, right, preferred_element_type=F32)


def m4(v):
    return lax.rem(v + 4, 4)


def m8(v):
    return lax.rem(v + 8, 8)


def kernel(
    tok, ups, wg, wu, wd, aa_in, ab_in, mem,
    lr_out, ig_out, abg_out,
    xb, wb, aa, ab, mb, gu, rr, lw, hc, sb, rb, pb,
    r1, r2, r3, r4, lr_own, lr_sib, lr_one, lrx, lry, cf, apart, azb, afin, abr,
    xr, xd, xs, xds, xl, w0r, w0s, zr, zs, aas, abs_, mrs, d2s, d2r, rsr, rss, lrr, lrs, azr, azs, afr, afs,
):
    dp = lax.axis_index("dp")
    tp = lax.axis_index("tensor")
    yl, z = lax.div(dp, 8), lax.rem(dp, 8)
    x, yh, c = lax.div(tp, 4), lax.rem(lax.div(tp, 2), 2), lax.rem(tp, 2)
    y = yh * 2 + yl

    def dev(x_, y_, z_, c_):
        return {"dp": lax.rem(y_, 2) * 8 + z_, "tensor": x_ * 4 + lax.div(y_, 2) * 2 + c_}

    def copy(src, dst, ssem, rsem, to):
        return pltpu.make_async_remote_copy(
            src_ref=src, dst_ref=dst, send_sem=ssem, recv_sem=rsem, device_id=to, device_id_type=MESH
        )

    sib = dev(x, y, z, 1 - c)
    other_y = yh * 2 + (1 - yl)
    pending = []

    def send(*args):
        descriptor = copy(*args)
        descriptor.start()
        pending.append(descriptor)

    def got(dst, rsem):
        copy(dst, dst, rsem, rsem, sib).wait_recv()

    barrier = pltpu.get_barrier_semaphore()
    partners = [sib, dev(x, other_y, z, 1 - c)]
    partners += [dev(m4(x + i), y, z, c) for i in (1, 2, 3)]
    partners += [dev(x, m4(y + i), z, c) for i in (1, 2, 3)]
    partners += [dev(x, y, m8(z + i), c) for i in range(1, 8)]
    for partner in partners:
        pl.semaphore_signal(barrier, inc=1, device_id=partner, device_id_type=MESH)
    pl.semaphore_wait(barrier, len(partners))

    kf, ks = yl * 8 + z, (1 - yl) * 8 + z
    home = c == yl
    mats = (wg, wu, wd)

    def w0(b, m):
        return mats[m].at[:, b * COLS:(b + 1) * COLS], wb.at[kf, :, m * COLS:(m + 1) * COLS]

    def w0_local(b, m):
        return pltpu.make_async_copy(*w0(b, m), w0r.at[0, m])

    def w0_near(b, m):
        return copy(*w0(b, m), w0s.at[b, m], w0r.at[0, m], sib)

    def w0_far(b, m):
        return copy(*w0(b, m), w0s.at[b, m], w0r.at[1, m], dev(x, yh * 2 + c, z, b))

    def ab_local(b):
        return pltpu.make_async_copy(ab_in.at[:, b * COLS:(b + 1) * COLS], ab, abs_.at[0])

    def ab_near(b):
        return copy(ab_in.at[:, b * COLS:(b + 1) * COLS], ab, abs_.at[1], abs_.at[0], sib)

    for b in (0, 1):
        @pl.when(home & (c == b))
        def _():
            for m in range(3):
                w0_local(b, m).start()

        @pl.when(home & (c != b))
        def _():
            for m in range(3):
                w0_near(b, m).start()

    sources = (tok, ups)

    def place(t, i, j):
        return (m4(x + i), m4(y + j)) if t == 0 else (m4(x + j), m4(y + i))

    def slot(t, i, j, rows=slice(0, ROWS), core=None):
        px, py = place(t, i, j)
        return xb.at[t, c if core is None else core, px, py, rows]

    def to(t, i, j):
        px, py = place(t, i, j)
        return dev(px, py, z, c)

    halves = (slice(0, ROWS // 2), slice(ROWS // 2, ROWS))
    counts = [0, 0]

    def xsend(t, src, dst, i, j, key):
        n = counts[t]
        counts[t] += 1
        send(src, dst, xs.at[t, n], xr.at[(t,) + key], to(t, i, j))

    def share(t, i, j, src=None):
        send(slot(t, i, j) if src is None else src, slot(t, i, j), xds.at[t, i, j], xd.at[t, i, j], sib)

    own_local = [pltpu.make_async_copy(sources[t], slot(t, 0, 0), xl.at[t]) for t in (0, 1)]
    for t in (0, 1):
        own_local[t].start()
    for t in (0, 1):
        xsend(t, sources[t], slot(t, 0, 0), 1, 0, (3, 0, 0))
        xsend(t, sources[t], slot(t, 0, 0), -1, 0, (1, 0, 0))

    for b in (0, 1):
        @pl.when(jnp.logical_not(home))
        def _():
            for m in range(3):
                w0_far(b, m).start()

        @pl.when(home & (c == b))
        def _():
            ab_local(b).start()

        @pl.when(home & (c != b))
        def _():
            ab_near(b).start()

    aa_copy = pltpu.make_async_copy(aa_in, aa, aas.at[0])
    aa_copy.start()
    send(mem, mb.at[yl], mrs.at[0], mrs.at[1], dev(x, other_y, z, c))
    mb[yl] = mem[...]

    def w0_wait(first, k):
        for m in range(3):
            ref = wb.at[k, :, m * COLS:(m + 1) * COLS]
            if first:
                @pl.when(home)
                def _():
                    pltpu.make_async_copy(ref, ref, w0r.at[0, m]).wait()

                @pl.when(jnp.logical_not(home))
                def _():
                    got(ref, w0r.at[0, m])
            else:
                got(ref, w0r.at[1, m])

    up_z, down_z = dev(x, y, m8(z + 1), c), dev(x, y, m8(z - 1), c)

    w0_wait(True, kf)
    send(wb.at[kf], wb.at[kf], zs.at[0, 0], zr.at[2], up_z)
    send(wb.at[kf], wb.at[kf], zs.at[1, 0], zr.at[3], down_z)

    for t in (0, 1):
        xsend(t, sources[t], slot(t, 0, 0), 0, 1, (0, 3, 0))
        xsend(t, sources[t], slot(t, 0, 0), 0, -1, (0, 1, 0))
        share(t, 0, 0, sources[t])

    def across(t, i):
        xsend(t, slot(t, i, 0), slot(t, i, 0), 0, 1, (i % 4, 3, 0))
        xsend(t, slot(t, i, 0), slot(t, i, 0), 0, -1, (i % 4, 1, 0))
        share(t, i, 0)

    for t in (0, 1):
        for i, step, half in ((3, 1, 0), (1, -1, 1)):
            got(slot(t, i, 0), xr.at[t, i, 0, 0])
            xsend(t, slot(t, i, 0, halves[half]), slot(t, i, 0, halves[half]), step, 0, (2, 0, half))
    for t in (0, 1):
        across(t, 3)
        across(t, 1)

    w0_wait(False, ks)
    send(wb.at[ks], wb.at[ks], zs.at[0, 1], zr.at[4], up_z)
    send(wb.at[ks], wb.at[ks], zs.at[1, 1], zr.at[5], down_z)

    for t in (0, 1):
        for half in (0, 1):
            got(slot(t, 2, 0, halves[half]), xr.at[t, 2, 0, half])
        across(t, 2)

    def block_of(i):
        j = i - 2
        distance = lax.div(j, 4) + 1
        kind = lax.rem(j, 4)
        down = lax.rem(kind, 2)
        second = jnp.where(i == 15, 1, lax.div(kind, 2))
        zz = m8(z + jnp.where(down == 1, distance, -distance))
        zz = jnp.where(i < 2, z, zz)
        second = jnp.where(i < 2, i, second)
        return jnp.where(second == 1, 1 - yl, yl) * 8 + zz

    def zcopy(i, down, later):
        k = block_of(jnp.int32(i))
        return copy(wb.at[k], wb.at[k], zs.at[down, i], zr.at[later], down_z if down else up_z)

    def zstep(i):
        got(wb.at[block_of(jnp.int32(i))], zr.at[i])
        down = (i - 2) % 2
        later = i + 4 if i <= 10 else 15
        if i <= 10 or i == 13:
            send(*[wb.at[block_of(jnp.int32(i))]] * 2, zs.at[down, i], zr.at[later], down_z if down else up_z)

    for i in (2, 3):
        zstep(i)

    def pass_on(t, i):
        got(slot(t, i, 3), xr.at[t, i, 3, 0])
        xsend(t, slot(t, i, 3, halves[0]), slot(t, i, 3, halves[0]), 0, 1, (i, 2, 0))
        share(t, i, 3)
        got(slot(t, i, 1), xr.at[t, i, 1, 0])
        xsend(t, slot(t, i, 1, halves[1]), slot(t, i, 1, halves[1]), 0, -1, (i, 2, 1))
        share(t, i, 1)

    for i in (0, 3, 1):
        for t in (0, 1):
            pass_on(t, i)
    for i in (4, 5):
        zstep(i)
    for t in (0, 1):
        pass_on(t, 2)
    for i in (6, 7):
        zstep(i)
    for i in (0, 3, 1, 2):
        for t in (0, 1):
            for half in (0, 1):
                got(slot(t, i, 2, halves[half]), xr.at[t, i, 2, half])
            share(t, i, 2)
    for t in (0, 1):
        own_local[t].wait()
        for i in range(4):
            for j in range(4):
                got(slot(t, i, j, core=1 - c), xd.at[t, i, j])
    aa_copy.wait()

    gu[...] = jnp.zeros_like(gu)
    rr[...] = jnp.zeros_like(rr)
    lw[...] = jnp.zeros_like(lw)

    def forward(i, carry):
        for e in range(8, 16):
            @pl.when(i == e)
            def _():
                got(wb.at[block_of(jnp.int32(e))], zr.at[e])
                if e <= 10 or e == 13:
                    zcopy(e, (e - 2) % 2, e + 4 if e <= 10 else 15).start()

        k = block_of(i)
        kx, ky, kc = lax.div(k, 4), lax.rem(lax.div(k, 2), 2) * 2, lax.rem(k, 2)
        t = xb[0, kc, kx, pl.ds(ky, 2)].reshape(2 * ROWS, BLK)
        u = xb[1, kc, kx, pl.ds(ky, 2)].reshape(2 * ROWS, BLK)
        gu[...] += dot(t, wb[k, :, 0:2 * COLS])
        rr[...] += dot(u, wb[k, :, 2 * COLS:3 * COLS])
        lw[...] += dot(t, aa[k])
        return carry

    lax.fori_loop(0, 16, forward, 0)

    @pl.when(home)
    def _():
        pltpu.make_async_copy(ab, ab, abs_.at[0]).wait()

    @pl.when(jnp.logical_not(home))
    def _():
        got(ab, abs_.at[0])

    step = 128
    eye = lax.broadcasted_iota(jnp.int32, (step, step), 0) == lax.broadcasted_iota(jnp.int32, (step, step), 1)
    for r in range(2 * ROWS // step):
        rows = slice(r * step, (r + 1) * step)
        b_g, b_u = ab[0:RANK], ab[RANK:2 * RANK]
        gate, up, readout = gu[rows, 0:COLS], gu[rows, COLS:2 * COLS], rr[rows]
        low = lw[rows].astype(BF16)
        pol_gate = gate + adapter_scale * dot(low[:, 0:RANK], b_g)
        pol_up = up + adapter_scale * dot(low[:, RANK:2 * RANK], b_u)
        sig = jax.nn.sigmoid(pol_gate)
        act = pol_gate * sig
        shift = act * pol_up - gate * jax.nn.sigmoid(gate) * up
        part = jnp.sum(shift * readout, axis=1, keepdims=True)
        lr_own[:, rows] = jnp.sum(jnp.where(eye, part, 0.0), axis=0, keepdims=True)
        scaled = readout * (1.0 / math.sqrt(D))
        h_gate = (scaled * pol_up * (sig * (1.0 + pol_gate * (1.0 - sig)))).astype(BF16)
        h_up = (scaled * act).astype(BF16)
        hc[rows, 0:COLS] = h_gate
        hc[rows, COLS:2 * COLS] = h_up
        hc[rows, 2 * COLS:2 * COLS + RANK] = (adapter_scale * nt(h_gate, b_g)).astype(BF16)
        hc[rows, 2 * COLS + RANK:2 * COLS + 2 * RANK] = (adapter_scale * nt(h_up, b_u)).astype(BF16)

    send(lr_own, lr_sib, lrs.at[0], lrr.at[0], sib)

    def product(j, core):
        k = j * 2 + core
        return nt(hc[:, 0:2 * COLS], wb[k, :, 0:2 * COLS]) + nt(hc[:, 2 * COLS:], aa[k])

    def to_sib(j):
        return copy(sb.at[j], rb.at[j], d2s.at[j], d2r.at[j], sib)

    def back_send(j, carry):
        sb[j] = product(j, 1 - c).astype(BF16).reshape(2, ROWS, BLK)
        to_sib(j).start()
        return carry

    lax.fori_loop(0, 8, back_send, 0)

    got(lr_sib, lrr.at[0])
    lr_one[...] = lr_own[...] + lr_sib[...]
    lrx[x] = lr_one[...]
    for i in (1, 2, 3):
        send(lr_one, lrx.at[x], lrs.at[i], lrr.at[i], dev(m4(x + i), y, z, c))

    def back_own(j, carry):
        total = product(j, c).reshape(2, ROWS, BLK)
        to_sib(j).wait_recv()
        pb[lax.div(j, 2), pl.ds(lax.rem(j, 2) * 2, 2)] = (total + rb[j].astype(F32)).astype(BF16)
        return carry

    lax.fori_loop(0, 8, back_own, 0)

    def piece(h, i, q, rows):
        p = m4((x if h == 0 else y) + i)
        return (p, q, rows) if h == 0 else (q, p, rows)

    def hop(h, i):
        return dev(m4(x + i), y, z, c) if h == 0 else dev(x, m4(y + i), z, c)

    low_q, high_q, all_q = slice(0, 2), slice(2, 4), slice(0, 4)
    part_rows = (slice(0, 128), slice(128, 256))
    quarter = ((slice(0, 64), slice(64, 128)), (slice(128, 192), slice(192, 256)))

    def ring(stage, h, d, src, dst, target):
        send(src, dst, rss.at[h, stage, d], rsr.at[h, stage, d], target)

    def fold(idx, ref):
        pb[idx] = (pb[idx].astype(F32) + ref[...].astype(F32)).astype(BF16)

    for h in (0, 1):
        for d, q in ((0, low_q), (1, high_q)):
            ring(0, h, d, pb.at[piece(h, 2, q, part_rows[h])], r1.at[h, d], hop(h, 1 - 2 * d))

    for i in (1, 2, 3):
        got(lrx.at[m4(x - i)], lrr.at[i])
    lr_two = ((lrx[0] + lrx[1]) + lrx[2]) + lrx[3]
    lry[y] = lr_two
    for i in (1, 2, 3):
        send(lry.at[y], lry.at[y], lrs.at[3 + i], lrr.at[3 + i], dev(x, m4(y + i), z, c))

    for h in (0, 1):
        for d, q in ((0, low_q), (1, high_q)):
            got(r1.at[h, d], rsr.at[h, 0, d])
            side = 1 - 2 * d
            fold(piece(h, side, q, part_rows[h]), r1.at[h, d])
            ring(1, h, d, pb.at[piece(h, side, all_q, part_rows[h])], r2.at[h, d], hop(h, side))

    for i in (1, 2, 3):
        got(lry.at[m4(y - i)], lrr.at[3 + i])
    lr_row = (((lry[0] + lry[1]) + lry[2]) + lry[3]) / math.sqrt(D)
    got(mb.at[1 - yl], mrs.at[1])
    eye2 = lax.broadcasted_iota(jnp.int32, (ROWS, ROWS), 0) == lax.broadcasted_iota(jnp.int32, (ROWS, ROWS), 1)

    def column(row):
        return jnp.sum(jnp.where(eye2, row, 0.0), axis=1, keepdims=True)

    for g in (0, 1):
        members = mb[g]
        pair = lax.shift_right_logical(members, 1)
        side_row = (1 - 2 * (members - 2 * pair)).astype(F32)
        pair_row = pair.astype(F32)
        lr_g = lr_row[:, g * ROWS:(g + 1) * ROWS]
        value = side_row * (jnp.exp(lr_g) + lr_g)
        same = column(pair_row) == pair_row
        margin = beta_coef * jnp.sum(jnp.where(same, value, 0.0), axis=1, keepdims=True)
        weight = -loss_scale * beta_coef * jax.nn.sigmoid(-margin)
        cf[g] = weight * column(side_row) * (jnp.exp(column(lr_g)) + 1.0)

        @pl.when(yl == g)
        def _():
            lr_out[...] = lr_g

    coeff = cf[...].reshape(2 * ROWS, 1)
    low_t = (lw[...].astype(BF16).astype(F32) * coeff).T.astype(BF16)
    g_part = adapter_scale * dot(low_t[0:RANK], hc[:, 0:COLS])
    u_part = adapter_scale * dot(low_t[RANK:2 * RANK], hc[:, COLS:2 * COLS])
    apart[:, 0] = g_part.reshape(8, 8, COLS)
    apart[:, 1] = u_part.reshape(8, 8, COLS)
    for i in range(1, 8):
        send(apart.at[m8(z + i)], azb.at[z], azs.at[i], azr.at[i], dev(x, y, m8(z + i), c))
    azb[z] = apart[z]

    for h in (0, 1):
        for d in (0, 1):
            got(r2.at[h, d], rsr.at[h, 1, d])
        idx = piece(h, 0, all_q, part_rows[h])
        pb[idx] = (pb[idx].astype(F32) + r2[h, 0].astype(F32) + r2[h, 1].astype(F32)).astype(BF16)

    def last(h, j, rows):
        return (x, m4(y + j), rows) if h == 0 else (m4(x + j), y, rows)

    for h in (0, 1):
        for d in (0, 1):
            ring(2, h, d, pb.at[last(h, 2, quarter[h][d])], r3.at[h, d], hop(1 - h, 1 - 2 * d))

    for i in range(1, 8):
        got(azb.at[m8(z - i)], azr.at[i])
    total = azb[0]
    for i in range(1, 8):
        total = total + azb[i]
    afin[...] = total

    def a_near():
        return copy(afin.at[yl], abr.at[c], afs.at[0], afr.at[c], sib)

    def a_far():
        return copy(afin.at[1 - yl], abr.at[c], afs.at[1], afr.at[c], dev(x, other_y, z, yl))

    a_far().start()

    @pl.when(home)
    def _():
        abr[c] = afin[yl]

    @pl.when(jnp.logical_not(home))
    def _():
        a_near().start()

    for h in (0, 1):
        for d in (0, 1):
            got(r3.at[h, d], rsr.at[h, 2, d])
            side = 1 - 2 * d
            fold(last(h, side, quarter[h][d]), r3.at[h, d])
            ring(3, h, d, pb.at[last(h, side, part_rows[h])], r4.at[h, d], hop(1 - h, side))

    for h in (0, 1):
        for d in (0, 1):
            got(r4.at[h, d], rsr.at[h, 3, d])
        rows = part_rows[h]
        grad = pb[x, y, rows].astype(F32) + r4[h, 0].astype(F32) + r4[h, 1].astype(F32)
        ig_out[rows, :] = (grad * cf[yl, rows]).astype(BF16)

    @pl.when(home)
    def _():
        got(abr.at[1 - c], afr.at[1 - c])

    @pl.when(jnp.logical_not(home))
    def _():
        got(abr.at[0], afr.at[0])
        got(abr.at[1], afr.at[1])

    abg_out[:, 0:COLS] = abr[0]
    abg_out[:, COLS:2 * COLS] = abr[1]

    for descriptor in pending:
        descriptor.wait_send()
    for e in (8, 9, 10, 13):
        zcopy(e, (e - 2) % 2, e + 4 if e <= 10 else 15).wait_send()

    def sent(j, carry):
        to_sib(j).wait_send()
        return carry

    lax.fori_loop(0, 8, sent, 0)
    a_far().wait_send()

    @pl.when(jnp.logical_not(home))
    def _():
        a_near().wait_send()

    for b in (0, 1):
        @pl.when(home & (c != b))
        def _():
            for m in range(3):
                w0_near(b, m).wait_send()
            ab_near(b).wait_send()

        @pl.when(jnp.logical_not(home))
        def _():
            for m in range(3):
                w0_far(b, m).wait_send()


def on_device(tokens, upstream, gate_weight, up_weight, down_weight, adapter_a, adapter_b, membership):
    vmem, dma = pltpu.VMEM, pltpu.SemaphoreType.DMA
    anywhere = pl.BlockSpec(memory_space=pl.ANY)
    inside = pl.BlockSpec(memory_space=pltpu.VMEM)
    log_ratio, input_grad, b_gradient = pl.pallas_call(
        kernel,
        out_shape=(
            jax.ShapeDtypeStruct((1, ROWS), F32),
            jax.ShapeDtypeStruct((ROWS, BLK), BF16),
            jax.ShapeDtypeStruct((8, 2 * COLS), F32),
        ),
        in_specs=[anywhere] * 7 + [inside],
        out_specs=(inside,) * 3,
        scratch_shapes=[
            vmem((2, 2, 4, 4, ROWS, BLK), BF16),
            vmem((16, BLK, 3 * COLS), BF16),
            vmem((16, BLK, 2 * RANK), BF16),
            vmem((2 * RANK, COLS), BF16),
            vmem((2, 1, ROWS), jnp.int32),
            vmem((2 * ROWS, 2 * COLS), F32),
            vmem((2 * ROWS, COLS), F32),
            vmem((2 * ROWS, 2 * RANK), F32),
            vmem((2 * ROWS, 2 * COLS + 2 * RANK), BF16),
            vmem((8, 2, ROWS, BLK), BF16),
            vmem((8, 2, ROWS, BLK), BF16),
            vmem((4, 4, ROWS, BLK), BF16),
            vmem((2, 2, 2, 128, BLK), BF16),
            vmem((2, 2, 4, 128, BLK), BF16),
            vmem((2, 2, 64, BLK), BF16),
            vmem((2, 2, 128, BLK), BF16),
            vmem((1, 2 * ROWS), F32),
            vmem((1, 2 * ROWS), F32),
            vmem((1, 2 * ROWS), F32),
            vmem((4, 1, 2 * ROWS), F32),
            vmem((4, 1, 2 * ROWS), F32),
            vmem((2, ROWS, 1), F32),
            vmem((8, 2, 8, COLS), F32),
            vmem((8, 2, 8, COLS), F32),
            vmem((2, 8, COLS), F32),
            vmem((2, 8, COLS), F32),
            dma((2, 4, 4, 2)),
            dma((2, 4, 4)),
            dma((2, 24)),
            dma((2, 4, 4)),
            dma((2,)),
            dma((2, 3)),
            dma((2, 3)),
            dma((16,)),
            dma((2, 16)),
            dma((1,)),
            dma((2,)),
            dma((2,)),
            dma((8,)),
            dma((8,)),
            dma((2, 4, 2)),
            dma((2, 4, 2)),
            dma((7,)),
            dma((7,)),
            dma((8,)),
            dma((8,)),
            dma((2,)),
            dma((2,)),
        ],
        compiler_params=pltpu.CompilerParams(
            collective_id=0, has_side_effects=True, vmem_limit_bytes=56 * 1024 * 1024
        ),
    )(
        tokens, upstream, gate_weight, up_weight, down_weight,
        adapter_a.reshape(16, BLK, 2 * RANK), adapter_b, membership.reshape(1, ROWS),
    )
    return log_ratio.reshape(ROWS), input_grad, b_gradient


def solution(mesh):
    placed = (
        P("dp", "tensor"),
        P("dp", "tensor"),
        P("dp", "tensor"),
        P("dp", "tensor"),
        P("dp", "tensor"),
        P(),
        P(None, "tensor"),
        P("dp"),
    )
    return jax.shard_map(
        on_device,
        mesh=mesh,
        in_specs=placed,
        out_specs=(P("dp"), P("dp", "tensor"), P("dp", "tensor")),
        check_vma=False,
    )
```

```python
import math

import jax
import jax.numpy as jnp
from jax import lax
from jax.experimental import pallas as pl
from jax.experimental.pallas import tpu as pltpu
from jax.sharding import PartitionSpec as P

MESH = pl.DeviceIdType.MESH
BF16 = jnp.bfloat16
F32 = jnp.float32

adapter_scale = 0.5
beta_coef = 0.5
loss_scale = 128.0

ROWS = 256
BLK = 320
COLS = 256
RANK = 64
W = 2 * RANK
D = 5120


def tn(left, right):
    return lax.dot_general(left, right, (((0,), (0,)), ((), ())), preferred_element_type=F32)


def nt(left, right):
    return lax.dot_general(left, right, (((1,), (1,)), ((), ())), preferred_element_type=F32)


def dot(left, right):
    return jnp.dot(left, right, preferred_element_type=F32)


def m4(v):
    return lax.rem(v + 4, 4)


def m8(v):
    return lax.rem(v + 8, 8)


def kernel(
    tok, ups, wg, wu, wd, aa_in, ab_in, mem,
    lr_out, ig_out, abg_out,
    xb, wb, ab, mb, gu, rr, hc, sb, rb, pb,
    r1, r2, r3, r4, r5, r6, lr_own, lr_sib, lr_one, lrx, lry, cf, apart, azb, afin, abr,
    xr, xd, xs, xds, xl, w0r, w0s, zr, zs, aas, abs_, mrs, d2s, d2r, rar, ras, rbr, rbs, rcr, rcs, lrr, lrs, azr, azs, afr, afs,
):
    dp = lax.axis_index("dp")
    tp = lax.axis_index("tensor")
    yl, z = lax.div(dp, 8), lax.rem(dp, 8)
    x, yh, c = lax.div(tp, 4), lax.rem(lax.div(tp, 2), 2), lax.rem(tp, 2)
    y = yh * 2 + yl

    def dev(x_, y_, z_, c_):
        return {"dp": lax.rem(y_, 2) * 8 + z_, "tensor": x_ * 4 + lax.div(y_, 2) * 2 + c_}

    def copy(src, dst, ssem, rsem, to):
        return pltpu.make_async_remote_copy(
            src_ref=src, dst_ref=dst, send_sem=ssem, recv_sem=rsem, device_id=to, device_id_type=MESH
        )

    sib = dev(x, y, z, 1 - c)
    other_y = yh * 2 + (1 - yl)
    pending = []

    def send(*args):
        descriptor = copy(*args)
        descriptor.start()
        pending.append(descriptor)

    def got(dst, rsem):
        copy(dst, dst, rsem, rsem, sib).wait_recv()

    barrier = pltpu.get_barrier_semaphore()
    partners = [sib, dev(x, other_y, z, 1 - c)]
    partners += [dev(m4(x + i), y, z, c) for i in (1, 2, 3)]
    partners += [dev(x, m4(y + i), z, c) for i in (1, 2, 3)]
    partners += [dev(x, y, m8(z + i), c) for i in range(1, 8)]
    for partner in partners:
        pl.semaphore_signal(barrier, inc=1, device_id=partner, device_id_type=MESH)
    pl.semaphore_wait(barrier, len(partners))

    kf, ks = yl * 8 + z, (1 - yl) * 8 + z
    home = c == yl
    mats = (wg, wu, wd)

    def w0(b, m):
        return mats[m].at[:, b * COLS:(b + 1) * COLS], wb.at[kf, :, W + m * COLS:W + (m + 1) * COLS]

    def w0_local(b, m):
        return pltpu.make_async_copy(*w0(b, m), w0r.at[0, m])

    def w0_near(b, m):
        return copy(*w0(b, m), w0s.at[b, m], w0r.at[0, m], sib)

    def w0_far(b, m):
        return copy(*w0(b, m), w0s.at[b, m], w0r.at[1, m], dev(x, yh * 2 + c, z, b))

    def ab_local(b):
        return pltpu.make_async_copy(ab_in.at[:, b * COLS:(b + 1) * COLS], ab, abs_.at[0])

    def ab_near(b):
        return copy(ab_in.at[:, b * COLS:(b + 1) * COLS], ab, abs_.at[1], abs_.at[0], sib)

    for b in (0, 1):
        @pl.when(home & (c == b))
        def _():
            for m in range(3):
                w0_local(b, m).start()

        @pl.when(home & (c != b))
        def _():
            for m in range(3):
                w0_near(b, m).start()

    sources = (tok, ups)

    def place(t, i, j):
        return (m4(x + i), m4(y + j)) if t == 0 else (m4(x + j), m4(y + i))

    def slot(t, i, j, rows=slice(0, BLK), core=None):
        px, py = place(t, i, j)
        return xb.at[t, c if core is None else core, px, py, rows]

    def to(t, i, j):
        px, py = place(t, i, j)
        return dev(px, py, z, c)

    halves = (slice(0, BLK // 2), slice(BLK // 2, BLK))
    counts = [0, 0]

    def xsend(t, src, dst, i, j, key):
        n = counts[t]
        counts[t] += 1
        send(src, dst, xs.at[t, n], xr.at[(t,) + key], to(t, i, j))

    def share(t, i, j, src=None):
        send(slot(t, i, j) if src is None else src, slot(t, i, j), xds.at[t, i, j], xd.at[t, i, j], sib)

    own_local = [pltpu.make_async_copy(sources[t], slot(t, 0, 0), xl.at[t]) for t in (0, 1)]
    for t in (0, 1):
        own_local[t].start()
    for t in (0, 1):
        xsend(t, sources[t], slot(t, 0, 0), 1, 0, (3, 0, 0))
        xsend(t, sources[t], slot(t, 0, 0), -1, 0, (1, 0, 0))

    for b in (0, 1):
        @pl.when(jnp.logical_not(home))
        def _():
            for m in range(3):
                w0_far(b, m).start()

        @pl.when(home & (c == b))
        def _():
            ab_local(b).start()

        @pl.when(home & (c != b))
        def _():
            ab_near(b).start()

    aa_copy = pltpu.make_async_copy(aa_in, wb.at[:, :, 0:W], aas.at[0])
    aa_copy.start()
    send(mem, mb.at[yl], mrs.at[0], mrs.at[1], dev(x, other_y, z, c))
    mb[yl] = mem[...]

    def weights(ref, k):
        return ref.at[k, :, W:W + 3 * COLS]

    def w0_wait(first, k):
        for m in range(3):
            ref = wb.at[k, :, W + m * COLS:W + (m + 1) * COLS]
            if first:
                @pl.when(home)
                def _():
                    pltpu.make_async_copy(ref, ref, w0r.at[0, m]).wait()

                @pl.when(jnp.logical_not(home))
                def _():
                    got(ref, w0r.at[0, m])
            else:
                got(ref, w0r.at[1, m])

    up_z, down_z = dev(x, y, m8(z + 1), c), dev(x, y, m8(z - 1), c)

    w0_wait(True, kf)
    send(weights(wb, kf), weights(wb, kf), zs.at[0, 0], zr.at[2], up_z)
    send(weights(wb, kf), weights(wb, kf), zs.at[1, 0], zr.at[3], down_z)

    for t in (0, 1):
        xsend(t, sources[t], slot(t, 0, 0), 0, 1, (0, 3, 0))
        xsend(t, sources[t], slot(t, 0, 0), 0, -1, (0, 1, 0))
        share(t, 0, 0, sources[t])

    def across(t, i):
        xsend(t, slot(t, i, 0), slot(t, i, 0), 0, 1, (i % 4, 3, 0))
        xsend(t, slot(t, i, 0), slot(t, i, 0), 0, -1, (i % 4, 1, 0))
        share(t, i, 0)

    for t in (0, 1):
        for i, step, half in ((3, 1, 0), (1, -1, 1)):
            got(slot(t, i, 0), xr.at[t, i, 0, 0])
            xsend(t, slot(t, i, 0, halves[half]), slot(t, i, 0, halves[half]), step, 0, (2, 0, half))
    for t in (0, 1):
        across(t, 3)
        across(t, 1)

    w0_wait(False, ks)
    send(weights(wb, ks), weights(wb, ks), zs.at[0, 1], zr.at[4], up_z)
    send(weights(wb, ks), weights(wb, ks), zs.at[1, 1], zr.at[5], down_z)

    for t in (0, 1):
        for half in (0, 1):
            got(slot(t, 2, 0, halves[half]), xr.at[t, 2, 0, half])
        across(t, 2)

    def block_of(i):
        j = i - 2
        distance = lax.div(j, 4) + 1
        kind = lax.rem(j, 4)
        down = lax.rem(kind, 2)
        second = jnp.where(i == 15, 1, lax.div(kind, 2))
        zz = m8(z + jnp.where(down == 1, distance, -distance))
        zz = jnp.where(i < 2, z, zz)
        second = jnp.where(i < 2, i, second)
        return jnp.where(second == 1, 1 - yl, yl) * 8 + zz

    def zcopy(i, down, later):
        k = block_of(jnp.int32(i))
        return copy(weights(wb, k), weights(wb, k), zs.at[down, i], zr.at[later], down_z if down else up_z)

    def zstep(i):
        got(weights(wb, block_of(jnp.int32(i))), zr.at[i])
        down = (i - 2) % 2
        later = i + 4 if i <= 10 else 15
        if i <= 10 or i == 13:
            send(*[weights(wb, block_of(jnp.int32(i)))] * 2, zs.at[down, i], zr.at[later], down_z if down else up_z)

    for i in (2, 3):
        zstep(i)

    def pass_on(t, i):
        got(slot(t, i, 3), xr.at[t, i, 3, 0])
        xsend(t, slot(t, i, 3, halves[0]), slot(t, i, 3, halves[0]), 0, 1, (i, 2, 0))
        share(t, i, 3)
        got(slot(t, i, 1), xr.at[t, i, 1, 0])
        xsend(t, slot(t, i, 1, halves[1]), slot(t, i, 1, halves[1]), 0, -1, (i, 2, 1))
        share(t, i, 1)

    for i in (0, 3, 1):
        for t in (0, 1):
            pass_on(t, i)
    for i in (4, 5):
        zstep(i)
    for t in (0, 1):
        pass_on(t, 2)
    for i in (6, 7):
        zstep(i)
    for i in (0, 3, 1, 2):
        for t in (0, 1):
            for half in (0, 1):
                got(slot(t, i, 2, halves[half]), xr.at[t, i, 2, half])
            share(t, i, 2)
    for t in (0, 1):
        own_local[t].wait()
        for i in range(4):
            for j in range(4):
                got(slot(t, i, j, core=1 - c), xd.at[t, i, j])
    aa_copy.wait()

    gu[...] = jnp.zeros_like(gu)
    rr[...] = jnp.zeros_like(rr)

    def forward(i, carry):
        for e in range(8, 16):
            @pl.when(i == e)
            def _():
                got(weights(wb, block_of(jnp.int32(e))), zr.at[e])
                if e <= 10 or e == 13:
                    zcopy(e, (e - 2) % 2, e + 4 if e <= 10 else 15).start()

        k = block_of(i)
        kx, ky, kc = lax.div(k, 4), lax.rem(lax.div(k, 2), 2) * 2, lax.rem(k, 2)
        t = jnp.concatenate([xb[0, kc, kx, ky], xb[0, kc, kx, ky + 1]], axis=1)
        u = jnp.concatenate([xb[1, kc, kx, ky], xb[1, kc, kx, ky + 1]], axis=1)
        gu[...] += tn(wb[k, :, 0:W + 2 * COLS], t)
        rr[...] += tn(wb[k, :, W + 2 * COLS:W + 3 * COLS], u)
        return carry

    lax.fori_loop(0, 16, forward, 0)

    @pl.when(home)
    def _():
        pltpu.make_async_copy(ab, ab, abs_.at[0]).wait()

    @pl.when(jnp.logical_not(home))
    def _():
        got(ab, abs_.at[0])

    low = gu[0:W].astype(BF16)
    b_t = ab[...].astype(F32).T.astype(BF16)
    step = 64
    ratio = jnp.zeros((1, 2 * ROWS), F32)
    for r in range(COLS // step):
        units = slice(r * step, (r + 1) * step)
        g_at, u_at = W + r * step, W + COLS + r * step
        gate, up, readout = gu[g_at:g_at + step], gu[u_at:u_at + step], rr[units]
        pol_gate = gate + adapter_scale * dot(b_t[units, 0:RANK], low[0:RANK])
        pol_up = up + adapter_scale * dot(b_t[units, RANK:W], low[RANK:W])
        sig = jax.nn.sigmoid(pol_gate)
        act = pol_gate * sig
        shift = act * pol_up - gate * jax.nn.sigmoid(gate) * up
        ratio += jnp.sum(shift * readout, axis=0, keepdims=True)
        scaled = readout * (1.0 / math.sqrt(D))
        hc[g_at:g_at + step] = (scaled * pol_up * (sig * (1.0 + pol_gate * (1.0 - sig)))).astype(BF16)
        hc[u_at:u_at + step] = (scaled * act).astype(BF16)
    lr_own[...] = ratio
    send(lr_own, lr_sib, lrs.at[0], lrr.at[0], sib)
    hc[0:RANK] = (adapter_scale * dot(ab[0:RANK], hc[W:W + COLS])).astype(BF16)
    hc[RANK:W] = (adapter_scale * dot(ab[RANK:W], hc[W + COLS:])).astype(BF16)

    first, second = slice(0, BLK // 2), slice(BLK // 2, BLK)

    def order(j):
        turn = lax.rem(j + 1, 3)
        dx = jnp.where(j < 2, 2, jnp.where(turn == 0, 1, jnp.where(turn == 1, 3, 0)))
        dh = jnp.where(j < 2, 1 - j, jnp.where(j < 5, 1, 0))
        return lax.rem(x + dx, 4), lax.rem(yh + dh, 2)

    def product(j, core):
        bx, bh = order(j)
        return dot(wb[bx * 4 + bh * 2 + core, :, 0:W + 2 * COLS], hc[...])

    def to_sib(j):
        return copy(sb.at[j], rb.at[j], d2s.at[j], d2r.at[j], sib)

    def back_send(j):
        sb[j] = product(j, 1 - c).astype(BF16)
        to_sib(j).start()

    up_x, down_x = dev(m4(x + 1), y, z, c), dev(m4(x - 1), y, z, c)
    up_y, down_y = dev(x, m4(y + 1), z, c), dev(x, m4(y - 1), z, c)
    far, near = (1 - yh) * 2, yh * 2
    pairs = (pl.ds(far, 2), pl.ds(near, 2))

    def fold(idx, ref):
        pb[idx] = (pb[idx].astype(F32) + ref[...].astype(F32)).astype(BF16)

    def a1(d):
        return copy(pb.at[m4(x + 2), pairs[d], first], r1.at[d], ras.at[0, d], rar.at[0, d], (up_x, down_x)[d])

    def a2(d, n):
        return copy(
            pb.at[m4(x + 1 - 2 * d), pairs[n], first], r2.at[d, n], ras.at[1 + n, d], rar.at[1 + n, d], (up_x, down_x)[d]
        )

    def a_fold(d):
        got(r1.at[d], rar.at[0, d])
        fold((m4(x + 1 - 2 * d), pairs[d], first), r1.at[d])

    def b_dir(dx):
        return 0 if dx in (1, 2) else 1

    def b1(dx):
        d = b_dir(dx)
        return copy(pb.at[m4(x + dx), m4(y + 2), second], r3.at[dx], rbs.at[0, dx], rbr.at[0, dx], (up_y, down_y)[d])

    def b2(dx, d):
        return copy(
            pb.at[m4(x + dx), m4(y + 1 - 2 * d), second], r4.at[d, dx], rbs.at[1 + d, dx], rbr.at[1 + d, dx], (up_y, down_y)[d]
        )

    def b_fold(dx):
        got(r3.at[dx], rbr.at[0, dx])
        fold((m4(x + dx), m4(y + 1 - 2 * b_dir(dx)), second), r3.at[dx])

    def b_both(dx):
        b_fold(dx)
        b2(dx, 0).start()
        b2(dx, 1).start()

    def after(j):
        if j == 0:
            a1(0).start()
            b1(2).start()
        elif j == 1:
            a1(1).start()
        elif j == 2:
            b1(1).start()
        elif j == 3:
            b1(3).start()
            a2(1, 0).start()
            a_fold(0)
            a2(0, 0).start()
        elif j == 4:
            b1(0).start()
            b_both(2)
        elif j == 5:
            a2(0, 1).start()
            b_both(1)
        elif j == 6:
            a_fold(1)
            a2(1, 1).start()
            b_both(3)
        else:
            b_both(0)

    back_send(0)

    def backward(j, carry):
        @pl.when(j < 7)
        def _():
            back_send(j + 1)

        total = product(j, c)
        to_sib(j).wait_recv()
        bx, bh = order(j)
        total = (total + rb[j].astype(F32)).astype(BF16)
        pb[bx, bh * 2] = total[:, 0:ROWS]
        pb[bx, bh * 2 + 1] = total[:, ROWS:]
        for e in range(8):
            @pl.when(j == e)
            def _():
                after(e)
                if e == 1:
                    got(lr_sib, lrr.at[0])
                    lr_one[...] = lr_own[...] + lr_sib[...]
                    lrx[x] = lr_one[...]
                    for i in (1, 2, 3):
                        copy(lr_one, lrx.at[x], lrs.at[i], lrr.at[i], dev(m4(x + i), y, z, c)).start()
                if e == 4:
                    for i in (1, 2, 3):
                        got(lrx.at[m4(x - i)], lrr.at[i])
                    lry[y] = ((lrx[0] + lrx[1]) + lrx[2]) + lrx[3]
                    for i in (1, 2, 3):
                        copy(lry.at[y], lry.at[y], lrs.at[3 + i], lrr.at[3 + i], dev(x, m4(y + i), z, c)).start()
        return carry

    lax.fori_loop(0, 8, backward, 0)

    for i in (1, 2, 3):
        got(lry.at[m4(y - i)], lrr.at[3 + i])
    lr_row = (((lry[0] + lry[1]) + lry[2]) + lry[3]) / math.sqrt(D)
    got(mb.at[1 - yl], mrs.at[1])
    eye2 = lax.broadcasted_iota(jnp.int32, (ROWS, ROWS), 0) == lax.broadcasted_iota(jnp.int32, (ROWS, ROWS), 1)

    def column(row):
        return jnp.sum(jnp.where(eye2, row, 0.0), axis=1, keepdims=True)

    for g in (0, 1):
        members = mb[g]
        pair = lax.shift_right_logical(members, 1)
        side = (1 - 2 * (members - 2 * pair)).astype(F32)
        pair = pair.astype(F32)
        lr_g = lr_row[:, g * ROWS:(g + 1) * ROWS]
        growth = jnp.exp(lr_g)
        same = column(pair) == pair
        margin = beta_coef * jnp.sum(jnp.where(same, column(side * (growth + lr_g)), 0.0), axis=0, keepdims=True)
        cf[g] = -loss_scale * beta_coef * jax.nn.sigmoid(-margin) * side * (growth + 1.0)

        @pl.when(yl == g)
        def _():
            lr_out[...] = lr_g

    low_t = (gu[0:W].astype(BF16).astype(F32) * jnp.concatenate([cf[0], cf[1]], axis=1)).astype(BF16)
    g_part = adapter_scale * nt(low_t[0:RANK], hc[W:W + COLS])
    u_part = adapter_scale * nt(low_t[RANK:W], hc[W + COLS:])
    apart[:, 0] = g_part.reshape(8, 8, COLS)
    apart[:, 1] = u_part.reshape(8, 8, COLS)
    for i in range(1, 8):
        send(apart.at[m8(z + i)], azb.at[z], azs.at[i], azr.at[i], dev(x, y, m8(z + i), c))
    azb[z] = apart[z]

    quarter = ((slice(0, 80), slice(80, 160)), (slice(160, 240), slice(240, 320)))

    def near_of(h, i):
        return (x, m4(y + i)) if h == 0 else (m4(x + i), y)

    ways = ((up_y, down_y), (up_x, down_x))

    def c1(h, d):
        return copy(pb.at[near_of(h, 2) + (quarter[h][d],)], r5.at[h, d], rcs.at[0, h, d], rcr.at[0, h, d], ways[h][d])

    def c2(h, d):
        rows = (first, second)[h]
        return copy(pb.at[near_of(h, 1 - 2 * d) + (rows,)], r6.at[h, d], rcs.at[1, h, d], rcr.at[1, h, d], ways[h][d])

    for n in (0, 1):
        for d in (0, 1):
            got(r2.at[d, n], rar.at[1 + n, d])
        idx = (x, pairs[n], first)
        pb[idx] = (pb[idx].astype(F32) + r2[0, n].astype(F32) + r2[1, n].astype(F32)).astype(BF16)
        if n == 0:
            for d in (0, 1):
                c1(0, d).start()
    for i in (2, 1, 3, 0):
        for d in (0, 1):
            got(r4.at[d, i], rbr.at[1 + d, i])
        idx = (m4(x + i), y, second)
        pb[idx] = (pb[idx].astype(F32) + r4[0, i].astype(F32) + r4[1, i].astype(F32)).astype(BF16)
        if i == 2:
            for d in (0, 1):
                c1(1, d).start()

    for i in range(1, 8):
        got(azb.at[m8(z - i)], azr.at[i])
    total = azb[0]
    for i in range(1, 8):
        total = total + azb[i]
    afin[...] = total

    def a_near():
        return copy(afin.at[yl], abr.at[c], afs.at[0], afr.at[c], sib)

    def a_far():
        return copy(afin.at[1 - yl], abr.at[c], afs.at[1], afr.at[c], dev(x, other_y, z, yl))

    a_far().start()

    @pl.when(home)
    def _():
        abr[c] = afin[yl]

    @pl.when(jnp.logical_not(home))
    def _():
        a_near().start()

    for h in (0, 1):
        for d in (0, 1):
            got(r5.at[h, d], rcr.at[0, h, d])
            fold(near_of(h, 1 - 2 * d) + (quarter[h][d],), r5.at[h, d])
            c2(h, d).start()

    for h in (0, 1):
        for d in (0, 1):
            got(r6.at[h, d], rcr.at[1, h, d])
        rows = (first, second)[h]
        grad = pb[x, y, rows].astype(F32) + r6[h, 0].astype(F32) + r6[h, 1].astype(F32)
        ig_out[rows, :] = (grad * cf[yl]).astype(BF16)

    @pl.when(home)
    def _():
        got(abr.at[1 - c], afr.at[1 - c])

    @pl.when(jnp.logical_not(home))
    def _():
        got(abr.at[0], afr.at[0])
        got(abr.at[1], afr.at[1])

    abg_out[:, 0:COLS] = abr[0]
    abg_out[:, COLS:2 * COLS] = abr[1]

    for descriptor in pending:
        descriptor.wait_send()
    for e in (8, 9, 10, 13):
        zcopy(e, (e - 2) % 2, e + 4 if e <= 10 else 15).wait_send()

    def sent(j, carry):
        to_sib(j).wait_send()
        return carry

    lax.fori_loop(0, 8, sent, 0)
    for d in (0, 1):
        a1(d).wait_send()
        for n in (0, 1):
            a2(d, n).wait_send()
        for dx in range(4):
            b2(dx, d).wait_send()
        for h in (0, 1):
            c1(h, d).wait_send()
            c2(h, d).wait_send()
    for dx in range(4):
        b1(dx).wait_send()
    for i in (1, 2, 3):
        copy(lr_one, lrx.at[x], lrs.at[i], lrr.at[i], dev(m4(x + i), y, z, c)).wait_send()
        copy(lry.at[y], lry.at[y], lrs.at[3 + i], lrr.at[3 + i], dev(x, m4(y + i), z, c)).wait_send()
    a_far().wait_send()

    @pl.when(jnp.logical_not(home))
    def _():
        a_near().wait_send()

    for b in (0, 1):
        @pl.when(home & (c != b))
        def _():
            for m in range(3):
                w0_near(b, m).wait_send()
            ab_near(b).wait_send()

        @pl.when(jnp.logical_not(home))
        def _():
            for m in range(3):
                w0_far(b, m).wait_send()


def on_device(tokens, upstream, gate_weight, up_weight, down_weight, adapter_a, adapter_b, membership):
    vmem, dma = pltpu.VMEM, pltpu.SemaphoreType.DMA
    anywhere = pl.BlockSpec(memory_space=pl.ANY)
    inside = pl.BlockSpec(memory_space=pltpu.VMEM)
    log_ratio, input_grad, b_gradient = pl.pallas_call(
        kernel,
        out_shape=(
            jax.ShapeDtypeStruct((1, ROWS), F32),
            jax.ShapeDtypeStruct((BLK, ROWS), BF16),
            jax.ShapeDtypeStruct((8, 2 * COLS), F32),
        ),
        in_specs=[anywhere] * 7 + [inside],
        out_specs=(inside,) * 3,
        scratch_shapes=[
            vmem((2, 2, 4, 4, BLK, ROWS), BF16),
            vmem((16, BLK, W + 3 * COLS), BF16),
            vmem((2 * RANK, COLS), BF16),
            vmem((2, 1, ROWS), jnp.int32),
            vmem((W + 2 * COLS, 2 * ROWS), F32),
            vmem((COLS, 2 * ROWS), F32),
            vmem((W + 2 * COLS, 2 * ROWS), BF16),
            vmem((8, BLK, 2 * ROWS), BF16),
            vmem((8, BLK, 2 * ROWS), BF16),
            vmem((4, 4, BLK, ROWS), BF16),
            vmem((2, 2, BLK // 2, ROWS), BF16),
            vmem((2, 2, 2, BLK // 2, ROWS), BF16),
            vmem((4, BLK // 2, ROWS), BF16),
            vmem((2, 4, BLK // 2, ROWS), BF16),
            vmem((2, 2, BLK // 4, ROWS), BF16),
            vmem((2, 2, BLK // 2, ROWS), BF16),
            vmem((1, 2 * ROWS), F32),
            vmem((1, 2 * ROWS), F32),
            vmem((1, 2 * ROWS), F32),
            vmem((4, 1, 2 * ROWS), F32),
            vmem((4, 1, 2 * ROWS), F32),
            vmem((2, 1, ROWS), F32),
            vmem((8, 2, 8, COLS), F32),
            vmem((8, 2, 8, COLS), F32),
            vmem((2, 8, COLS), F32),
            vmem((2, 8, COLS), F32),
            dma((2, 4, 4, 2)),
            dma((2, 4, 4)),
            dma((2, 24)),
            dma((2, 4, 4)),
            dma((2,)),
            dma((2, 3)),
            dma((2, 3)),
            dma((16,)),
            dma((2, 16)),
            dma((1,)),
            dma((2,)),
            dma((2,)),
            dma((8,)),
            dma((8,)),
            dma((3, 2)),
            dma((3, 2)),
            dma((3, 4)),
            dma((3, 4)),
            dma((2, 2, 2)),
            dma((2, 2, 2)),
            dma((7,)),
            dma((7,)),
            dma((8,)),
            dma((8,)),
            dma((2,)),
            dma((2,)),
        ],
        compiler_params=pltpu.CompilerParams(
            collective_id=0, has_side_effects=True, vmem_limit_bytes=56 * 1024 * 1024
        ),
    )(
        tokens.T, upstream.T, gate_weight, up_weight, down_weight,
        adapter_a.reshape(16, BLK, 2 * RANK), adapter_b, membership.reshape(1, ROWS),
    )
    return log_ratio.reshape(ROWS), input_grad.T, b_gradient


def solution(mesh):
    placed = (
        P("dp", "tensor"),
        P("dp", "tensor"),
        P("dp", "tensor"),
        P("dp", "tensor"),
        P("dp", "tensor"),
        P(),
        P(None, "tensor"),
        P("dp"),
    )
    return jax.shard_map(
        on_device,
        mesh=mesh,
        in_specs=placed,
        out_specs=(P("dp"), P("dp", "tensor"), P("dp", "tensor")),
        check_vma=False,
    )
```

```python
import math

import jax
import jax.numpy as jnp
from jax import lax
from jax.experimental import pallas as pl
from jax.experimental.pallas import tpu as pltpu
from jax.sharding import PartitionSpec as P

MESH = pl.DeviceIdType.MESH
BF16 = jnp.bfloat16
F32 = jnp.float32

adapter_scale = 0.5
beta_coef = 0.5
loss_scale = 128.0

ROWS = 256
BLK = 320
COLS = 256
RANK = 64
W = 2 * RANK
D = 5120


def tn(left, right):
    return lax.dot_general(left, right, (((0,), (0,)), ((), ())), preferred_element_type=F32)


def nt(left, right):
    return lax.dot_general(left, right, (((1,), (1,)), ((), ())), preferred_element_type=F32)


def dot(left, right):
    return jnp.dot(left, right, preferred_element_type=F32)


def m4(v):
    return lax.rem(v + 4, 4)


def m8(v):
    return lax.rem(v + 8, 8)


def kernel(
    tok, ups, wg, wu, wd, aa_in, ab_in, mem,
    lr_out, ig_out, abg_out,
    xb, wb, ab, mb, gu, rr, hc, sb, rb, pb,
    r1, r2, r3, r4, r5, r6, lr_own, lr_sib, lr_one, lrx, lry, cf, apart, azb, afin, abr,
    xr, xd, xs, xds, xl, w0r, w0s, zr, zs, aas, abs_, mrs, d2s, d2r, rar, ras, rbr, rbs, rcr, rcs, lrr, lrs, azr, azs, afr, afs,
):
    dp = lax.axis_index("dp")
    tp = lax.axis_index("tensor")
    yl, z = lax.div(dp, 8), lax.rem(dp, 8)
    x, yh, c = lax.div(tp, 4), lax.rem(lax.div(tp, 2), 2), lax.rem(tp, 2)
    y = yh * 2 + yl

    def dev(x_, y_, z_, c_):
        return {"dp": lax.rem(y_, 2) * 8 + z_, "tensor": x_ * 4 + lax.div(y_, 2) * 2 + c_}

    def copy(src, dst, ssem, rsem, to):
        return pltpu.make_async_remote_copy(
            src_ref=src, dst_ref=dst, send_sem=ssem, recv_sem=rsem, device_id=to, device_id_type=MESH
        )

    sib = dev(x, y, z, 1 - c)
    other_y = yh * 2 + (1 - yl)
    pending = []

    def send(*args):
        descriptor = copy(*args)
        descriptor.start()
        pending.append(descriptor)

    def got(dst, rsem):
        copy(dst, dst, rsem, rsem, sib).wait_recv()

    barrier = pltpu.get_barrier_semaphore()
    partners = [sib, dev(x, other_y, z, 1 - c)]
    partners += [dev(m4(x + i), y, z, c) for i in (1, 2, 3)]
    partners += [dev(x, m4(y + i), z, c) for i in (1, 2, 3)]
    partners += [dev(x, y, m8(z + i), c) for i in range(1, 8)]
    for partner in partners:
        pl.semaphore_signal(barrier, inc=1, device_id=partner, device_id_type=MESH)
    pl.semaphore_wait(barrier, len(partners))

    kf, ks = yl * 8 + z, (1 - yl) * 8 + z
    home = c == yl
    mats = (wg, wu, wd)

    def w0(b, m):
        return mats[m].at[:, b * COLS:(b + 1) * COLS], wb.at[kf, :, W + m * COLS:W + (m + 1) * COLS]

    def w0_local(b, m):
        return pltpu.make_async_copy(*w0(b, m), w0r.at[0, m])

    def w0_near(b, m):
        return copy(*w0(b, m), w0s.at[b, m], w0r.at[0, m], sib)

    def w0_far(b, m):
        return copy(*w0(b, m), w0s.at[b, m], w0r.at[1, m], dev(x, yh * 2 + c, z, b))

    def ab_local(b):
        return pltpu.make_async_copy(ab_in.at[:, b * COLS:(b + 1) * COLS], ab, abs_.at[0])

    def ab_near(b):
        return copy(ab_in.at[:, b * COLS:(b + 1) * COLS], ab, abs_.at[1], abs_.at[0], sib)

    for b in (0, 1):
        @pl.when(home & (c == b))
        def _():
            for m in range(3):
                w0_local(b, m).start()

        @pl.when(home & (c != b))
        def _():
            for m in range(3):
                w0_near(b, m).start()

    sources = (tok, ups)

    def place(t, i, j):
        return (m4(x + i), m4(y + j)) if t == 0 else (m4(x + j), m4(y + i))

    def slot(t, i, j, rows=slice(0, BLK), core=None):
        px, py = place(t, i, j)
        return xb.at[t, c if core is None else core, px, py, rows]

    def to(t, i, j):
        px, py = place(t, i, j)
        return dev(px, py, z, c)

    halves = (slice(0, BLK // 2), slice(BLK // 2, BLK))
    counts = [0, 0]

    def xsend(t, src, dst, i, j, key):
        n = counts[t]
        counts[t] += 1
        send(src, dst, xs.at[t, n], xr.at[(t,) + key], to(t, i, j))

    def share(t, i, j, src=None):
        send(slot(t, i, j) if src is None else src, slot(t, i, j), xds.at[t, i, j], xd.at[t, i, j], sib)

    own_local = [pltpu.make_async_copy(sources[t], slot(t, 0, 0), xl.at[t]) for t in (0, 1)]
    for t in (0, 1):
        own_local[t].start()
    for t in (0, 1):
        xsend(t, sources[t], slot(t, 0, 0), 1, 0, (3, 0, 0))
        xsend(t, sources[t], slot(t, 0, 0), -1, 0, (1, 0, 0))

    for b in (0, 1):
        @pl.when(jnp.logical_not(home))
        def _():
            for m in range(3):
                w0_far(b, m).start()

        @pl.when(home & (c == b))
        def _():
            ab_local(b).start()

        @pl.when(home & (c != b))
        def _():
            ab_near(b).start()

    aa_copy = pltpu.make_async_copy(aa_in, wb.at[:, :, 0:W], aas.at[0])
    aa_copy.start()
    send(mem, mb.at[yl], mrs.at[0], mrs.at[1], dev(x, other_y, z, c))
    mb[yl] = mem[...]

    def weights(ref, k):
        return ref.at[k, :, W:W + 3 * COLS]

    def w0_wait(first, k):
        for m in range(3):
            ref = wb.at[k, :, W + m * COLS:W + (m + 1) * COLS]
            if first:
                @pl.when(home)
                def _():
                    pltpu.make_async_copy(ref, ref, w0r.at[0, m]).wait()

                @pl.when(jnp.logical_not(home))
                def _():
                    got(ref, w0r.at[0, m])
            else:
                got(ref, w0r.at[1, m])

    up_z, down_z = dev(x, y, m8(z + 1), c), dev(x, y, m8(z - 1), c)

    w0_wait(True, kf)
    send(weights(wb, kf), weights(wb, kf), zs.at[0, 0], zr.at[2], up_z)
    send(weights(wb, kf), weights(wb, kf), zs.at[1, 0], zr.at[3], down_z)

    for t in (0, 1):
        xsend(t, sources[t], slot(t, 0, 0), 0, 1, (0, 3, 0))
        xsend(t, sources[t], slot(t, 0, 0), 0, -1, (0, 1, 0))
        share(t, 0, 0, sources[t])

    def across(t, i):
        xsend(t, slot(t, i, 0), slot(t, i, 0), 0, 1, (i % 4, 3, 0))
        xsend(t, slot(t, i, 0), slot(t, i, 0), 0, -1, (i % 4, 1, 0))
        share(t, i, 0)

    for t in (0, 1):
        for i, step, half in ((3, 1, 0), (1, -1, 1)):
            got(slot(t, i, 0), xr.at[t, i, 0, 0])
            xsend(t, slot(t, i, 0, halves[half]), slot(t, i, 0, halves[half]), step, 0, (2, 0, half))
    for t in (0, 1):
        across(t, 3)
        across(t, 1)

    w0_wait(False, ks)
    send(weights(wb, ks), weights(wb, ks), zs.at[0, 1], zr.at[4], up_z)
    send(weights(wb, ks), weights(wb, ks), zs.at[1, 1], zr.at[5], down_z)

    for t in (0, 1):
        for half in (0, 1):
            got(slot(t, 2, 0, halves[half]), xr.at[t, 2, 0, half])
        across(t, 2)

    def block_of(i):
        j = i - 2
        distance = lax.div(j, 4) + 1
        kind = lax.rem(j, 4)
        down = lax.rem(kind, 2)
        second = jnp.where(i == 15, 1, lax.div(kind, 2))
        zz = m8(z + jnp.where(down == 1, distance, -distance))
        zz = jnp.where(i < 2, z, zz)
        second = jnp.where(i < 2, i, second)
        return jnp.where(second == 1, 1 - yl, yl) * 8 + zz

    def zcopy(i, down, later):
        k = block_of(jnp.int32(i))
        return copy(weights(wb, k), weights(wb, k), zs.at[down, i], zr.at[later], down_z if down else up_z)

    def zstep(i):
        got(weights(wb, block_of(jnp.int32(i))), zr.at[i])
        down = (i - 2) % 2
        later = i + 4 if i <= 10 else 15
        if i <= 10 or i == 13:
            send(*[weights(wb, block_of(jnp.int32(i)))] * 2, zs.at[down, i], zr.at[later], down_z if down else up_z)

    for i in (2, 3):
        zstep(i)

    def pass_on(t, i):
        got(slot(t, i, 3), xr.at[t, i, 3, 0])
        xsend(t, slot(t, i, 3, halves[0]), slot(t, i, 3, halves[0]), 0, 1, (i, 2, 0))
        share(t, i, 3)
        got(slot(t, i, 1), xr.at[t, i, 1, 0])
        xsend(t, slot(t, i, 1, halves[1]), slot(t, i, 1, halves[1]), 0, -1, (i, 2, 1))
        share(t, i, 1)

    for i in (0, 3, 1):
        for t in (0, 1):
            pass_on(t, i)
    for i in (4, 5):
        zstep(i)
    for t in (0, 1):
        pass_on(t, 2)
    for i in (6, 7):
        zstep(i)
    for i in (0, 3, 1, 2):
        for t in (0, 1):
            for half in (0, 1):
                got(slot(t, i, 2, halves[half]), xr.at[t, i, 2, half])
            share(t, i, 2)
    for t in (0, 1):
        own_local[t].wait()
        for i in range(4):
            for j in range(4):
                got(slot(t, i, j, core=1 - c), xd.at[t, i, j])
    aa_copy.wait()

    gu[...] = jnp.zeros_like(gu)
    rr[...] = jnp.zeros_like(rr)

    def forward(i, carry):
        for e in range(8, 16):
            @pl.when(i == e)
            def _():
                got(weights(wb, block_of(jnp.int32(e))), zr.at[e])
                if e <= 10 or e == 13:
                    zcopy(e, (e - 2) % 2, e + 4 if e <= 10 else 15).start()

        k = block_of(i)
        kx, ky, kc = lax.div(k, 4), lax.rem(lax.div(k, 2), 2) * 2, lax.rem(k, 2)
        t = jnp.concatenate([xb[0, kc, kx, ky], xb[0, kc, kx, ky + 1]], axis=1)
        u = jnp.concatenate([xb[1, kc, kx, ky], xb[1, kc, kx, ky + 1]], axis=1)
        gu[...] += tn(wb[k, :, 0:W + 2 * COLS], t)
        rr[...] += tn(wb[k, :, W + 2 * COLS:W + 3 * COLS], u)
        return carry

    lax.fori_loop(0, 16, forward, 0)

    @pl.when(home)
    def _():
        pltpu.make_async_copy(ab, ab, abs_.at[0]).wait()

    @pl.when(jnp.logical_not(home))
    def _():
        got(ab, abs_.at[0])

    low = gu[0:W].astype(BF16)
    b_t = ab[...].astype(F32).T.astype(BF16)
    step = 64
    ratio = jnp.zeros((1, 2 * ROWS), F32)
    for r in range(COLS // step):
        units = slice(r * step, (r + 1) * step)
        g_at, u_at = W + r * step, W + COLS + r * step
        gate, up, readout = gu[g_at:g_at + step], gu[u_at:u_at + step], rr[units]
        pol_gate = gate + adapter_scale * dot(b_t[units, 0:RANK], low[0:RANK])
        pol_up = up + adapter_scale * dot(b_t[units, RANK:W], low[RANK:W])
        sig = jax.nn.sigmoid(pol_gate)
        act = pol_gate * sig
        shift = act * pol_up - gate * jax.nn.sigmoid(gate) * up
        ratio += jnp.sum(shift * readout, axis=0, keepdims=True)
        scaled = readout * (1.0 / math.sqrt(D))
        hc[g_at:g_at + step] = (scaled * pol_up * (sig * (1.0 + pol_gate * (1.0 - sig)))).astype(BF16)
        hc[u_at:u_at + step] = (scaled * act).astype(BF16)
    lr_own[...] = ratio
    send(lr_own, lr_sib, lrs.at[0], lrr.at[0], sib)
    hc[0:RANK] = (adapter_scale * dot(ab[0:RANK], hc[W:W + COLS])).astype(BF16)
    hc[RANK:W] = (adapter_scale * dot(ab[RANK:W], hc[W + COLS:])).astype(BF16)

    first, second = slice(0, BLK // 2), slice(BLK // 2, BLK)

    def order(j):
        turn = lax.rem(j + 1, 3)
        dx = jnp.where(j < 2, 2, jnp.where(turn == 0, 1, jnp.where(turn == 1, 3, 0)))
        dh = jnp.where(j < 2, 1 - j, jnp.where(j < 5, 1, 0))
        return lax.rem(x + dx, 4), lax.rem(yh + dh, 2)

    def product(j, core):
        bx, bh = order(j)
        return dot(wb[bx * 4 + bh * 2 + core, :, 0:W + 2 * COLS], hc[...])

    def to_sib(j):
        return copy(sb.at[j], rb.at[j], d2s.at[j], d2r.at[j], sib)

    def back_send(j):
        sb[j] = product(j, 1 - c).astype(BF16)
        to_sib(j).start()

    up_x, down_x = dev(m4(x + 1), y, z, c), dev(m4(x - 1), y, z, c)
    up_y, down_y = dev(x, m4(y + 1), z, c), dev(x, m4(y - 1), z, c)
    far, near = (1 - yh) * 2, yh * 2
    pairs = (pl.ds(far, 2), pl.ds(near, 2))

    def fold(idx, ref):
        pb[idx] = (pb[idx].astype(F32) + ref[...].astype(F32)).astype(BF16)

    def a1(d):
        return copy(pb.at[m4(x + 2), pairs[d], first], r1.at[d], ras.at[0, d], rar.at[0, d], (up_x, down_x)[d])

    def a2(d, n):
        return copy(
            pb.at[m4(x + 1 - 2 * d), pairs[n], first], r2.at[d, n], ras.at[1 + n, d], rar.at[1 + n, d], (up_x, down_x)[d]
        )

    def a_fold(d):
        got(r1.at[d], rar.at[0, d])
        fold((m4(x + 1 - 2 * d), pairs[d], first), r1.at[d])

    def b_dir(dx):
        return 0 if dx in (1, 2) else 1

    def b1(dx):
        d = b_dir(dx)
        return copy(pb.at[m4(x + dx), m4(y + 2), second], r3.at[dx], rbs.at[0, dx], rbr.at[0, dx], (up_y, down_y)[d])

    def b2(dx, d):
        return copy(
            pb.at[m4(x + dx), m4(y + 1 - 2 * d), second], r4.at[d, dx], rbs.at[1 + d, dx], rbr.at[1 + d, dx], (up_y, down_y)[d]
        )

    def b_fold(dx):
        got(r3.at[dx], rbr.at[0, dx])
        fold((m4(x + dx), m4(y + 1 - 2 * b_dir(dx)), second), r3.at[dx])

    def b_both(dx):
        b_fold(dx)
        b2(dx, 0).start()
        b2(dx, 1).start()

    def after(j):
        if j == 0:
            a1(0).start()
            b1(2).start()
        elif j == 1:
            a1(1).start()
        elif j == 2:
            b1(1).start()
        elif j == 3:
            b1(3).start()
            a2(1, 0).start()
            a_fold(0)
            a2(0, 0).start()
        elif j == 4:
            b1(0).start()
            b_both(2)
        elif j == 5:
            a2(0, 1).start()
            b_both(1)
        elif j == 6:
            a_fold(1)
            a2(1, 1).start()
            b_both(3)
        else:
            b_both(0)

    back_send(0)

    def backward(j, carry):
        @pl.when(j < 7)
        def _():
            back_send(j + 1)

        total = product(j, c)
        to_sib(j).wait_recv()
        bx, bh = order(j)
        total = (total + rb[j].astype(F32)).astype(BF16)
        pb[bx, bh * 2] = total[:, 0:ROWS]
        pb[bx, bh * 2 + 1] = total[:, ROWS:]
        for e in range(8):
            @pl.when(j == e)
            def _():
                after(e)
                if e == 1:
                    got(lr_sib, lrr.at[0])
                    lr_one[...] = lr_own[...] + lr_sib[...]
                    lrx[x] = lr_one[...]
                    for i in (1, 2, 3):
                        copy(lr_one, lrx.at[x], lrs.at[i], lrr.at[i], dev(m4(x + i), y, z, c)).start()
                if e == 4:
                    for i in (1, 2, 3):
                        got(lrx.at[m4(x - i)], lrr.at[i])
                    lry[y] = ((lrx[0] + lrx[1]) + lrx[2]) + lrx[3]
                    for i in (1, 2, 3):
                        copy(lry.at[y], lry.at[y], lrs.at[3 + i], lrr.at[3 + i], dev(x, m4(y + i), z, c)).start()
        return carry

    lax.fori_loop(0, 8, backward, 0)

    for i in (1, 2, 3):
        got(lry.at[m4(y - i)], lrr.at[3 + i])
    lr_row = (((lry[0] + lry[1]) + lry[2]) + lry[3]) / math.sqrt(D)
    got(mb.at[1 - yl], mrs.at[1])
    eye2 = lax.broadcasted_iota(jnp.int32, (ROWS, ROWS), 0) == lax.broadcasted_iota(jnp.int32, (ROWS, ROWS), 1)

    def column(row):
        return jnp.sum(jnp.where(eye2, row, 0.0), axis=1, keepdims=True)

    for g in (0, 1):
        members = mb[g]
        pair = lax.shift_right_logical(members, 1)
        side = (1 - 2 * (members - 2 * pair)).astype(F32)
        pair = pair.astype(F32)
        lr_g = lr_row[:, g * ROWS:(g + 1) * ROWS]
        growth = jnp.exp(lr_g)
        same = column(pair) == pair
        margin = beta_coef * jnp.sum(jnp.where(same, column(side * (growth + lr_g)), 0.0), axis=0, keepdims=True)
        cf[g] = -loss_scale * beta_coef * jax.nn.sigmoid(-margin) * side * (growth + 1.0)

        @pl.when(yl == g)
        def _():
            lr_out[...] = lr_g

    low_t = (gu[0:W].astype(BF16).astype(F32) * jnp.concatenate([cf[0], cf[1]], axis=1)).astype(BF16)
    g_part = adapter_scale * nt(low_t[0:RANK], hc[W:W + COLS])
    u_part = adapter_scale * nt(low_t[RANK:W], hc[W + COLS:])
    apart[:, 0] = g_part.reshape(8, 8, COLS)
    apart[:, 1] = u_part.reshape(8, 8, COLS)
    for i in range(1, 8):
        send(apart.at[m8(z + i)], azb.at[z], azs.at[i], azr.at[i], dev(x, y, m8(z + i), c))
    azb[z] = apart[z]

    quarter = ((slice(0, 80), slice(80, 160)), (slice(160, 240), slice(240, 320)))

    def near_of(h, i):
        return (x, m4(y + i)) if h == 0 else (m4(x + i), y)

    ways = ((up_y, down_y), (up_x, down_x))

    def c1(h, d):
        return copy(pb.at[near_of(h, 2) + (quarter[h][d],)], r5.at[h, d], rcs.at[0, h, d], rcr.at[0, h, d], ways[h][d])

    def c2(h, d):
        rows = (first, second)[h]
        return copy(pb.at[near_of(h, 1 - 2 * d) + (rows,)], r6.at[h, d], rcs.at[1, h, d], rcr.at[1, h, d], ways[h][d])

    for n in (0, 1):
        for d in (0, 1):
            got(r2.at[d, n], rar.at[1 + n, d])
        idx = (x, pairs[n], first)
        pb[idx] = (pb[idx].astype(F32) + r2[0, n].astype(F32) + r2[1, n].astype(F32)).astype(BF16)
        if n == 0:
            for d in (0, 1):
                c1(0, d).start()
    for i in (2, 1, 3, 0):
        for d in (0, 1):
            got(r4.at[d, i], rbr.at[1 + d, i])
        idx = (m4(x + i), y, second)
        pb[idx] = (pb[idx].astype(F32) + r4[0, i].astype(F32) + r4[1, i].astype(F32)).astype(BF16)
        if i == 2:
            for d in (0, 1):
                c1(1, d).start()

    for i in range(1, 8):
        got(azb.at[m8(z - i)], azr.at[i])
    total = azb[0]
    for i in range(1, 8):
        total = total + azb[i]
    afin[...] = total

    def a_near():
        return copy(afin.at[yl], abr.at[c], afs.at[0], afr.at[c], sib)

    def a_far():
        return copy(afin.at[1 - yl], abr.at[c], afs.at[1], afr.at[c], dev(x, other_y, z, yl))

    a_far().start()

    @pl.when(home)
    def _():
        abr[c] = afin[yl]

    @pl.when(jnp.logical_not(home))
    def _():
        a_near().start()

    for h in (0, 1):
        for d in (0, 1):
            got(r5.at[h, d], rcr.at[0, h, d])
            fold(near_of(h, 1 - 2 * d) + (quarter[h][d],), r5.at[h, d])
            c2(h, d).start()

    for h in (0, 1):
        for d in (0, 1):
            got(r6.at[h, d], rcr.at[1, h, d])
        rows = (first, second)[h]
        grad = pb[x, y, rows].astype(F32) + r6[h, 0].astype(F32) + r6[h, 1].astype(F32)
        ig_out[rows, :] = (grad * cf[yl]).astype(BF16)

    @pl.when(home)
    def _():
        got(abr.at[1 - c], afr.at[1 - c])

    @pl.when(jnp.logical_not(home))
    def _():
        got(abr.at[0], afr.at[0])
        got(abr.at[1], afr.at[1])

    abg_out[:, 0:COLS] = abr[0]
    abg_out[:, COLS:2 * COLS] = abr[1]

    for descriptor in pending:
        descriptor.wait_send()
    for e in (8, 9, 10, 13):
        zcopy(e, (e - 2) % 2, e + 4 if e <= 10 else 15).wait_send()

    def sent(j, carry):
        to_sib(j).wait_send()
        return carry

    lax.fori_loop(0, 8, sent, 0)
    for d in (0, 1):
        a1(d).wait_send()
        for n in (0, 1):
            a2(d, n).wait_send()
        for dx in range(4):
            b2(dx, d).wait_send()
        for h in (0, 1):
            c1(h, d).wait_send()
            c2(h, d).wait_send()
    for dx in range(4):
        b1(dx).wait_send()
    for i in (1, 2, 3):
        copy(lr_one, lrx.at[x], lrs.at[i], lrr.at[i], dev(m4(x + i), y, z, c)).wait_send()
        copy(lry.at[y], lry.at[y], lrs.at[3 + i], lrr.at[3 + i], dev(x, m4(y + i), z, c)).wait_send()
    a_far().wait_send()

    @pl.when(jnp.logical_not(home))
    def _():
        a_near().wait_send()

    for b in (0, 1):
        @pl.when(home & (c != b))
        def _():
            for m in range(3):
                w0_near(b, m).wait_send()
            ab_near(b).wait_send()

        @pl.when(jnp.logical_not(home))
        def _():
            for m in range(3):
                w0_far(b, m).wait_send()


def hand_on(lr_in, ig_in, abg_in, lr_out, ig_out, abg_out):
    lr_out[...] = lr_in[0]
    ig_out[...] = ig_in[...]
    abg_out[...] = abg_in[...]


def on_device(tokens, upstream, gate_weight, up_weight, down_weight, adapter_a, adapter_b, membership):
    vmem, dma = pltpu.VMEM, pltpu.SemaphoreType.DMA
    anywhere = pl.BlockSpec(memory_space=pl.ANY)
    inside = pl.BlockSpec(memory_space=pltpu.VMEM)
    log_ratio, input_grad, b_gradient = pl.pallas_call(
        kernel,
        out_shape=(
            jax.ShapeDtypeStruct((1, ROWS), F32),
            jax.ShapeDtypeStruct((BLK, ROWS), BF16),
            jax.ShapeDtypeStruct((8, 2 * COLS), F32),
        ),
        in_specs=[anywhere] * 7 + [inside],
        out_specs=(inside,) * 3,
        scratch_shapes=[
            vmem((2, 2, 4, 4, BLK, ROWS), BF16),
            vmem((16, BLK, W + 3 * COLS), BF16),
            vmem((2 * RANK, COLS), BF16),
            vmem((2, 1, ROWS), jnp.int32),
            vmem((W + 2 * COLS, 2 * ROWS), F32),
            vmem((COLS, 2 * ROWS), F32),
            vmem((W + 2 * COLS, 2 * ROWS), BF16),
            vmem((8, BLK, 2 * ROWS), BF16),
            vmem((8, BLK, 2 * ROWS), BF16),
            vmem((4, 4, BLK, ROWS), BF16),
            vmem((2, 2, BLK // 2, ROWS), BF16),
            vmem((2, 2, 2, BLK // 2, ROWS), BF16),
            vmem((4, BLK // 2, ROWS), BF16),
            vmem((2, 4, BLK // 2, ROWS), BF16),
            vmem((2, 2, BLK // 4, ROWS), BF16),
            vmem((2, 2, BLK // 2, ROWS), BF16),
            vmem((1, 2 * ROWS), F32),
            vmem((1, 2 * ROWS), F32),
            vmem((1, 2 * ROWS), F32),
            vmem((4, 1, 2 * ROWS), F32),
            vmem((4, 1, 2 * ROWS), F32),
            vmem((2, 1, ROWS), F32),
            vmem((8, 2, 8, COLS), F32),
            vmem((8, 2, 8, COLS), F32),
            vmem((2, 8, COLS), F32),
            vmem((2, 8, COLS), F32),
            dma((2, 4, 4, 2)),
            dma((2, 4, 4)),
            dma((2, 24)),
            dma((2, 4, 4)),
            dma((2,)),
            dma((2, 3)),
            dma((2, 3)),
            dma((16,)),
            dma((2, 16)),
            dma((1,)),
            dma((2,)),
            dma((2,)),
            dma((8,)),
            dma((8,)),
            dma((3, 2)),
            dma((3, 2)),
            dma((3, 4)),
            dma((3, 4)),
            dma((2, 2, 2)),
            dma((2, 2, 2)),
            dma((7,)),
            dma((7,)),
            dma((8,)),
            dma((8,)),
            dma((2,)),
            dma((2,)),
        ],
        compiler_params=pltpu.CompilerParams(
            collective_id=0, has_side_effects=True, vmem_limit_bytes=56 * 1024 * 1024
        ),
    )(
        tokens.T, upstream.T, gate_weight, up_weight, down_weight,
        adapter_a.reshape(16, BLK, 2 * RANK), adapter_b, membership.reshape(1, ROWS),
    )
    log_ratio, input_grad, b_gradient = pl.pallas_call(
        hand_on,
        out_shape=(
            jax.ShapeDtypeStruct((ROWS,), F32),
            jax.ShapeDtypeStruct((BLK, ROWS), BF16),
            jax.ShapeDtypeStruct((8, 2 * COLS), F32),
        ),
        in_specs=[inside] * 3,
        out_specs=(inside,) * 3,
    )(log_ratio, input_grad, b_gradient)
    return log_ratio, input_grad.T, b_gradient


def solution(mesh):
    placed = (
        P("dp", "tensor"),
        P("dp", "tensor"),
        P("dp", "tensor"),
        P("dp", "tensor"),
        P("dp", "tensor"),
        P(),
        P(None, "tensor"),
        P("dp"),
    )
    return jax.shard_map(
        on_device,
        mesh=mesh,
        in_specs=placed,
        out_specs=(P("dp"), P("dp", "tensor"), P("dp", "tensor")),
        check_vma=False,
    )
```

```python
import math

import jax
import jax.numpy as jnp
from jax import lax
from jax.experimental import pallas as pl
from jax.experimental.pallas import tpu as pltpu
from jax.sharding import PartitionSpec as P

MESH = pl.DeviceIdType.MESH
BF16 = jnp.bfloat16
F32 = jnp.float32

adapter_scale = 0.5
beta_coef = 0.5
loss_scale = 128.0

ROWS = 256
BLK = 320
COLS = 256
RANK = 64
W = 2 * RANK
D = 5120
CUT = 176


def tn(left, right):
    return lax.dot_general(left, right, (((0,), (0,)), ((), ())), preferred_element_type=F32)


def nt(left, right):
    return lax.dot_general(left, right, (((1,), (1,)), ((), ())), preferred_element_type=F32)


def dot(left, right):
    return jnp.dot(left, right, preferred_element_type=F32)


def m4(v):
    return lax.rem(v + 4, 4)


def m8(v):
    return lax.rem(v + 8, 8)


def kernel(
    tok, ups, wg, wu, wd, aa_in, ab_in, mem,
    lr_out, ig_out, abg_out,
    xb, wb, ab, mb, gu, rr, hc, sb, rb, pb,
    r1, r2, r3, r4, r5, r6, lr_own, lrx, lry, cf, apart, azb, afin, abr,
    xr, xd, xs, xds, xl, w0r, w0s, zr, zs, aas, abs_, mrs, d2s, d2r, rar, ras, rbr, rbs, rcr, rcs, lrr, lrs, azr, azs, afr, afs,
):
    dp = lax.axis_index("dp")
    tp = lax.axis_index("tensor")
    yl, z = lax.div(dp, 8), lax.rem(dp, 8)
    x, yh, c = lax.div(tp, 4), lax.rem(lax.div(tp, 2), 2), lax.rem(tp, 2)
    y = yh * 2 + yl

    def dev(x_, y_, z_, c_):
        return {"dp": lax.rem(y_, 2) * 8 + z_, "tensor": x_ * 4 + lax.div(y_, 2) * 2 + c_}

    def copy(src, dst, ssem, rsem, to):
        return pltpu.make_async_remote_copy(
            src_ref=src, dst_ref=dst, send_sem=ssem, recv_sem=rsem, device_id=to, device_id_type=MESH
        )

    sib = dev(x, y, z, 1 - c)
    other_y = yh * 2 + (1 - yl)
    pending = []

    def send(*args):
        descriptor = copy(*args)
        descriptor.start()
        pending.append(descriptor)

    def got(dst, rsem):
        copy(dst, dst, rsem, rsem, sib).wait_recv()

    barrier = pltpu.get_barrier_semaphore()
    partners = [sib, dev(x, other_y, z, 1 - c)]
    partners += [dev(m4(x + i), y, z, c) for i in (1, 2, 3)]
    partners += [dev(m4(x + i), y, z, 1 - c) for i in (1, 2, 3)]
    partners += [dev(x, m4(y + i), z, c) for i in (1, 2, 3)]
    partners += [dev(x, y, m8(z + i), c) for i in range(1, 8)]
    for partner in partners:
        pl.semaphore_signal(barrier, inc=1, device_id=partner, device_id_type=MESH)
    pl.semaphore_wait(barrier, len(partners))

    kf, ks = yl * 8 + z, (1 - yl) * 8 + z
    home = c == yl
    mats = (wg, wu, wd)

    def w0(b, m):
        return mats[m].at[:, b * COLS:(b + 1) * COLS], wb.at[kf, :, W + m * COLS:W + (m + 1) * COLS]

    def w0_local(b, m):
        return pltpu.make_async_copy(*w0(b, m), w0r.at[0, m])

    def w0_near(b, m):
        return copy(*w0(b, m), w0s.at[b, m], w0r.at[0, m], sib)

    def w0_far(b, m):
        return copy(*w0(b, m), w0s.at[b, m], w0r.at[1, m], dev(x, yh * 2 + c, z, b))

    def ab_local(b):
        return pltpu.make_async_copy(ab_in.at[:, b * COLS:(b + 1) * COLS], ab, abs_.at[0])

    def ab_near(b):
        return copy(ab_in.at[:, b * COLS:(b + 1) * COLS], ab, abs_.at[1], abs_.at[0], sib)

    for b in (0, 1):
        @pl.when(home & (c == b))
        def _():
            for m in range(3):
                w0_local(b, m).start()

        @pl.when(home & (c != b))
        def _():
            for m in range(3):
                w0_near(b, m).start()

    sources = (tok, ups)

    def place(t, i, j):
        return (m4(x + i), m4(y + j)) if t == 0 else (m4(x + j), m4(y + i))

    def slot(t, i, j, rows=slice(0, BLK), core=None):
        px, py = place(t, i, j)
        return xb.at[t, c if core is None else core, px, py, rows]

    def to(t, i, j):
        px, py = place(t, i, j)
        return dev(px, py, z, c)

    halves = (slice(0, BLK // 2), slice(BLK // 2, BLK))
    counts = [0, 0]

    def xsend(t, src, dst, i, j, key):
        n = counts[t]
        counts[t] += 1
        send(src, dst, xs.at[t, n], xr.at[(t,) + key], to(t, i, j))

    def share(t, i, j, src=None):
        send(slot(t, i, j) if src is None else src, slot(t, i, j), xds.at[t, i, j], xd.at[t, i, j], sib)

    own_local = [pltpu.make_async_copy(sources[t], slot(t, 0, 0), xl.at[t]) for t in (0, 1)]
    for t in (0, 1):
        own_local[t].start()
    for t in (0, 1):
        xsend(t, sources[t], slot(t, 0, 0), 1, 0, (3, 0, 0))
        xsend(t, sources[t], slot(t, 0, 0), -1, 0, (1, 0, 0))

    for b in (0, 1):
        @pl.when(jnp.logical_not(home))
        def _():
            for m in range(3):
                w0_far(b, m).start()

        @pl.when(home & (c == b))
        def _():
            ab_local(b).start()

        @pl.when(home & (c != b))
        def _():
            ab_near(b).start()

    aa_copy = pltpu.make_async_copy(aa_in, wb.at[:, :, 0:W], aas.at[0])
    aa_copy.start()
    send(mem, mb.at[yl], mrs.at[0], mrs.at[1], dev(x, other_y, z, c))
    mb[yl] = mem[...]

    def weights(ref, k):
        return ref.at[k, :, W:W + 3 * COLS]

    def w0_wait(first, k):
        for m in range(3):
            ref = wb.at[k, :, W + m * COLS:W + (m + 1) * COLS]
            if first:
                @pl.when(home)
                def _():
                    pltpu.make_async_copy(ref, ref, w0r.at[0, m]).wait()

                @pl.when(jnp.logical_not(home))
                def _():
                    got(ref, w0r.at[0, m])
            else:
                got(ref, w0r.at[1, m])

    up_z, down_z = dev(x, y, m8(z + 1), c), dev(x, y, m8(z - 1), c)

    w0_wait(True, kf)
    send(weights(wb, kf), weights(wb, kf), zs.at[0, 0], zr.at[2], up_z)
    send(weights(wb, kf), weights(wb, kf), zs.at[1, 0], zr.at[3], down_z)

    for t in (0, 1):
        xsend(t, sources[t], slot(t, 0, 0), 0, 1, (0, 3, 0))
        xsend(t, sources[t], slot(t, 0, 0), 0, -1, (0, 1, 0))
        share(t, 0, 0, sources[t])

    def across(t, i):
        xsend(t, slot(t, i, 0), slot(t, i, 0), 0, 1, (i % 4, 3, 0))
        xsend(t, slot(t, i, 0), slot(t, i, 0), 0, -1, (i % 4, 1, 0))
        share(t, i, 0)

    for t in (0, 1):
        for i, step, half in ((3, 1, 0), (1, -1, 1)):
            got(slot(t, i, 0), xr.at[t, i, 0, 0])
            xsend(t, slot(t, i, 0, halves[half]), slot(t, i, 0, halves[half]), step, 0, (2, 0, half))
    for t in (0, 1):
        across(t, 3)
        across(t, 1)

    w0_wait(False, ks)
    send(weights(wb, ks), weights(wb, ks), zs.at[0, 1], zr.at[4], up_z)
    send(weights(wb, ks), weights(wb, ks), zs.at[1, 1], zr.at[5], down_z)

    for t in (0, 1):
        for half in (0, 1):
            got(slot(t, 2, 0, halves[half]), xr.at[t, 2, 0, half])
        across(t, 2)

    def block_of(i):
        j = i - 2
        distance = lax.div(j, 4) + 1
        kind = lax.rem(j, 4)
        down = lax.rem(kind, 2)
        second = jnp.where(i == 15, 1, lax.div(kind, 2))
        zz = m8(z + jnp.where(down == 1, distance, -distance))
        zz = jnp.where(i < 2, z, zz)
        second = jnp.where(i < 2, i, second)
        return jnp.where(second == 1, 1 - yl, yl) * 8 + zz

    def zcopy(i, down, later):
        k = block_of(jnp.int32(i))
        return copy(weights(wb, k), weights(wb, k), zs.at[down, i], zr.at[later], down_z if down else up_z)

    def zstep(i):
        got(weights(wb, block_of(jnp.int32(i))), zr.at[i])
        down = (i - 2) % 2
        later = i + 4 if i <= 10 else 15
        if i <= 10 or i == 13:
            send(*[weights(wb, block_of(jnp.int32(i)))] * 2, zs.at[down, i], zr.at[later], down_z if down else up_z)

    for i in (2, 3):
        zstep(i)

    def pass_on(t, i):
        got(slot(t, i, 3), xr.at[t, i, 3, 0])
        xsend(t, slot(t, i, 3, halves[0]), slot(t, i, 3, halves[0]), 0, 1, (i, 2, 0))
        share(t, i, 3)
        got(slot(t, i, 1), xr.at[t, i, 1, 0])
        xsend(t, slot(t, i, 1, halves[1]), slot(t, i, 1, halves[1]), 0, -1, (i, 2, 1))
        share(t, i, 1)

    for i in (0, 3, 1):
        for t in (0, 1):
            pass_on(t, i)
    for i in (4, 5):
        zstep(i)
    for t in (0, 1):
        pass_on(t, 2)
    for i in (6, 7):
        zstep(i)
    for i in (0, 3, 1, 2):
        for t in (0, 1):
            for half in (0, 1):
                got(slot(t, i, 2, halves[half]), xr.at[t, i, 2, half])
            share(t, i, 2)
    for t in (0, 1):
        own_local[t].wait()
        for i in range(4):
            for j in range(4):
                got(slot(t, i, j, core=1 - c), xd.at[t, i, j])
    aa_copy.wait()

    gu[...] = jnp.zeros_like(gu)
    rr[...] = jnp.zeros_like(rr)

    def forward(i, carry):
        for e in range(8, 16):
            @pl.when(i == e)
            def _():
                got(weights(wb, block_of(jnp.int32(e))), zr.at[e])
                if e <= 10 or e == 13:
                    zcopy(e, (e - 2) % 2, e + 4 if e <= 10 else 15).start()

        k = block_of(i)
        kx, ky, kc = lax.div(k, 4), lax.rem(lax.div(k, 2), 2) * 2, lax.rem(k, 2)
        t = jnp.concatenate([xb[0, kc, kx, ky], xb[0, kc, kx, ky + 1]], axis=1)
        u = jnp.concatenate([xb[1, kc, kx, ky], xb[1, kc, kx, ky + 1]], axis=1)
        gu[...] += tn(wb[k, :, 0:W + 2 * COLS], t)
        rr[...] += tn(wb[k, :, W + 2 * COLS:W + 3 * COLS], u)
        return carry

    lax.fori_loop(0, 16, forward, 0)

    @pl.when(home)
    def _():
        pltpu.make_async_copy(ab, ab, abs_.at[0]).wait()

    @pl.when(jnp.logical_not(home))
    def _():
        got(ab, abs_.at[0])

    low = gu[0:W].astype(BF16)
    b_t = ab[...].astype(F32).T.astype(BF16)
    step = 64
    ratio = jnp.zeros((1, 2 * ROWS), F32)
    for r in range(COLS // step):
        units = slice(r * step, (r + 1) * step)
        g_at, u_at = W + r * step, W + COLS + r * step
        gate, up, readout = gu[g_at:g_at + step], gu[u_at:u_at + step], rr[units]
        pol_gate = gate + adapter_scale * dot(b_t[units, 0:RANK], low[0:RANK])
        pol_up = up + adapter_scale * dot(b_t[units, RANK:W], low[RANK:W])
        sig = jax.nn.sigmoid(pol_gate)
        act = pol_gate * sig
        shift = act * pol_up - gate * jax.nn.sigmoid(gate) * up
        ratio += jnp.sum(shift * readout, axis=0, keepdims=True)
        scaled = readout * (1.0 / math.sqrt(D))
        hc[g_at:g_at + step] = (scaled * pol_up * (sig * (1.0 + pol_gate * (1.0 - sig)))).astype(BF16)
        hc[u_at:u_at + step] = (scaled * act).astype(BF16)
    lr_own[...] = ratio
    lrx[x, c] = ratio
    around = [(i, f) for i in range(4) for f in (0, 1) if i or f]

    def lr_send(i, f):
        n, core = 2 * i + f, 1 - c if f else c
        return copy(lr_own, lrx.at[x, c], lrs.at[n], lrr.at[n], dev(m4(x + i), y, z, core))

    def lr_send_y(i):
        return copy(lry.at[y], lry.at[y], lrs.at[7 + i], lrr.at[7 + i], dev(x, m4(y + i), z, c))

    for i, f in around:
        lr_send(i, f).start()
    hc[0:RANK] = (adapter_scale * dot(ab[0:RANK], hc[W:W + COLS])).astype(BF16)
    hc[RANK:W] = (adapter_scale * dot(ab[RANK:W], hc[W + COLS:])).astype(BF16)

    first, second = slice(0, CUT), slice(CUT, BLK)

    def order(j):
        turn = lax.rem(j + 1, 3)
        dx = jnp.where(j < 2, 2, jnp.where(turn == 0, 1, jnp.where(turn == 1, 3, 0)))
        dh = jnp.where(j < 2, 1 - j, jnp.where(j < 5, 1, 0))
        return lax.rem(x + dx, 4), lax.rem(yh + dh, 2)

    def product(j, core):
        bx, bh = order(j)
        return dot(wb[bx * 4 + bh * 2 + core, :, 0:W + 2 * COLS], hc[...])

    def to_sib(j):
        return copy(sb.at[j], rb.at[j], d2s.at[j], d2r.at[j], sib)

    def back_send(j):
        sb[j] = product(j, 1 - c).astype(BF16)
        to_sib(j).start()

    up_x, down_x = dev(m4(x + 1), y, z, c), dev(m4(x - 1), y, z, c)
    up_y, down_y = dev(x, m4(y + 1), z, c), dev(x, m4(y - 1), z, c)
    far, near = (1 - yh) * 2, yh * 2
    pairs = (pl.ds(far, 2), pl.ds(near, 2))

    def fold(idx, ref):
        pb[idx] = (pb[idx].astype(F32) + ref[...].astype(F32)).astype(BF16)

    def a1(d):
        return copy(pb.at[m4(x + 2), pairs[d], first], r1.at[d], ras.at[0, d], rar.at[0, d], (up_x, down_x)[d])

    def a2(d, n):
        return copy(
            pb.at[m4(x + 1 - 2 * d), pairs[n], first], r2.at[d, n], ras.at[1 + n, d], rar.at[1 + n, d], (up_x, down_x)[d]
        )

    def a_fold(d):
        got(r1.at[d], rar.at[0, d])
        fold((m4(x + 1 - 2 * d), pairs[d], first), r1.at[d])

    def b_dir(dx):
        return 0 if dx in (1, 2) else 1

    def b1(dx):
        d = b_dir(dx)
        return copy(pb.at[m4(x + dx), m4(y + 2), second], r3.at[dx], rbs.at[0, dx], rbr.at[0, dx], (up_y, down_y)[d])

    def b2(dx, d):
        return copy(
            pb.at[m4(x + dx), m4(y + 1 - 2 * d), second], r4.at[d, dx], rbs.at[1 + d, dx], rbr.at[1 + d, dx], (up_y, down_y)[d]
        )

    def b_fold(dx):
        got(r3.at[dx], rbr.at[0, dx])
        fold((m4(x + dx), m4(y + 1 - 2 * b_dir(dx)), second), r3.at[dx])

    def b_both(dx):
        b_fold(dx)
        b2(dx, 0).start()
        b2(dx, 1).start()

    def after(j):
        if j == 0:
            a1(0).start()
            b1(2).start()
        elif j == 1:
            a1(1).start()
        elif j == 2:
            b1(1).start()
        elif j == 3:
            b1(3).start()
            a2(1, 0).start()
            a_fold(0)
            a2(0, 0).start()
        elif j == 4:
            b1(0).start()
            b_both(2)
        elif j == 5:
            a2(0, 1).start()
            b_both(1)
        elif j == 6:
            a_fold(1)
            a2(1, 1).start()
            b_both(3)
        else:
            b_both(0)

    def az_send(i):
        return copy(apart.at[m8(z + i)], azb.at[z], azs.at[i], azr.at[i], dev(x, y, m8(z + i), c))

    def coefficients():
        for i in (1, 2, 3):
            got(lry.at[m4(y - i)], lrr.at[7 + i])
        lr_row = (((lry[0] + lry[1]) + lry[2]) + lry[3]) / math.sqrt(D)
        got(mb.at[1 - yl], mrs.at[1])
        eye2 = lax.broadcasted_iota(jnp.int32, (ROWS, ROWS), 0) == lax.broadcasted_iota(jnp.int32, (ROWS, ROWS), 1)

        def column(row):
            return jnp.sum(jnp.where(eye2, row, 0.0), axis=1, keepdims=True)

        for g in (0, 1):
            members = mb[g]
            pair = lax.shift_right_logical(members, 1)
            side = (1 - 2 * (members - 2 * pair)).astype(F32)
            pair = pair.astype(F32)
            lr_g = lr_row[:, g * ROWS:(g + 1) * ROWS]
            growth = jnp.exp(lr_g)
            same = column(pair) == pair
            margin = beta_coef * jnp.sum(jnp.where(same, column(side * (growth + lr_g)), 0.0), axis=0, keepdims=True)
            cf[g] = -loss_scale * beta_coef * jax.nn.sigmoid(-margin) * side * (growth + 1.0)

            @pl.when(yl == g)
            def _():
                lr_out[...] = lr_g

        low_t = (gu[0:W].astype(BF16).astype(F32) * jnp.concatenate([cf[0], cf[1]], axis=1)).astype(BF16)
        g_part = adapter_scale * nt(low_t[0:RANK], hc[W:W + COLS])
        u_part = adapter_scale * nt(low_t[RANK:W], hc[W + COLS:])
        apart[:, 0] = g_part.reshape(8, 8, COLS)
        apart[:, 1] = u_part.reshape(8, 8, COLS)
        for i in range(1, 8):
            az_send(i).start()
        azb[z] = apart[z]

    def a_near():
        return copy(afin.at[yl], abr.at[c], afs.at[0], afr.at[c], sib)

    def a_far():
        return copy(afin.at[1 - yl], abr.at[c], afs.at[1], afr.at[c], dev(x, other_y, z, yl))

    def hand_out():
        for i in range(1, 8):
            got(azb.at[m8(z - i)], azr.at[i])
        total = azb[0]
        for i in range(1, 8):
            total = total + azb[i]
        afin[...] = total

        a_far().start()

        @pl.when(home)
        def _():
            abr[c] = afin[yl]

        @pl.when(jnp.logical_not(home))
        def _():
            a_near().start()

    def log_ratios():
        for i, f in around:
            got(lrx.at[m4(x - i), 1 - c if f else c], lrr.at[2 * i + f])
        rows = [lrx[i, 0] + lrx[i, 1] for i in range(4)]
        lry[y] = ((rows[0] + rows[1]) + rows[2]) + rows[3]
        for i in (1, 2, 3):
            lr_send_y(i).start()

    back_send(0)

    def backward(j, carry):
        @pl.when(j < 7)
        def _():
            back_send(j + 1)

        total = product(j, c)
        to_sib(j).wait_recv()
        bx, bh = order(j)
        total = (total + rb[j].astype(F32)).astype(BF16)
        pb[bx, bh * 2] = total[:, 0:ROWS]
        pb[bx, bh * 2 + 1] = total[:, ROWS:]
        for e in range(8):
            @pl.when(j == e)
            def _():
                after(e)
                if e == 1:
                    log_ratios()
                if e == 5:
                    coefficients()
        return carry

    lax.fori_loop(0, 8, backward, 0)

    quarter = ((slice(0, 96), slice(96, CUT)), (slice(CUT, 256), slice(256, BLK)))
    size = ((96, CUT - 96), (256 - CUT, BLK - 256))
    span = (CUT, BLK - CUT)

    def near_of(h, i):
        return (x, m4(y + i)) if h == 0 else (m4(x + i), y)

    ways = ((up_y, down_y), (up_x, down_x))

    def c1(h, d):
        return copy(pb.at[near_of(h, 2) + (quarter[h][d],)], r5.at[h, d, 0:size[h][d]], rcs.at[0, h, d], rcr.at[0, h, d], ways[h][d])

    def c2(h, d):
        rows = (first, second)[h]
        return copy(pb.at[near_of(h, 1 - 2 * d) + (rows,)], r6.at[h, d, 0:span[h]], rcs.at[1, h, d], rcr.at[1, h, d], ways[h][d])

    def x_sum(n):
        for d in (0, 1):
            got(r2.at[d, n], rar.at[1 + n, d])
        idx = (x, pairs[n], first)
        pb[idx] = (pb[idx].astype(F32) + r2[0, n].astype(F32) + r2[1, n].astype(F32)).astype(BF16)

    def y_sum(i):
        for d in (0, 1):
            got(r4.at[d, i], rbr.at[1 + d, i])
        idx = (m4(x + i), y, second)
        pb[idx] = (pb[idx].astype(F32) + r4[0, i].astype(F32) + r4[1, i].astype(F32)).astype(BF16)

    def second_hop(h):
        for d in (0, 1):
            got(r5.at[h, d, 0:size[h][d]], rcr.at[0, h, d])
            fold(near_of(h, 1 - 2 * d) + (quarter[h][d],), r5.at[h, d, 0:size[h][d]])
            c2(h, d).start()

    x_sum(0)
    for d in (0, 1):
        c1(0, d).start()
    y_sum(2)
    for d in (0, 1):
        c1(1, d).start()
    x_sum(1)
    y_sum(1)
    second_hop(0)
    y_sum(3)
    second_hop(1)
    y_sum(0)
    hand_out()

    for h in (0, 1):
        for d in (0, 1):
            got(r6.at[h, d, 0:span[h]], rcr.at[1, h, d])
        rows = (first, second)[h]
        grad = pb[x, y, rows].astype(F32) + r6[h, 0, 0:span[h]].astype(F32) + r6[h, 1, 0:span[h]].astype(F32)
        ig_out[rows, :] = (grad * cf[yl]).astype(BF16)

    @pl.when(home)
    def _():
        got(abr.at[1 - c], afr.at[1 - c])

    @pl.when(jnp.logical_not(home))
    def _():
        got(abr.at[0], afr.at[0])
        got(abr.at[1], afr.at[1])

    abg_out[:, 0:COLS] = abr[0]
    abg_out[:, COLS:2 * COLS] = abr[1]

    for descriptor in pending:
        descriptor.wait_send()
    for e in (8, 9, 10, 13):
        zcopy(e, (e - 2) % 2, e + 4 if e <= 10 else 15).wait_send()

    def sent(j, carry):
        to_sib(j).wait_send()
        return carry

    lax.fori_loop(0, 8, sent, 0)
    for d in (0, 1):
        a1(d).wait_send()
        for n in (0, 1):
            a2(d, n).wait_send()
        for dx in range(4):
            b2(dx, d).wait_send()
        for h in (0, 1):
            c1(h, d).wait_send()
            c2(h, d).wait_send()
    for dx in range(4):
        b1(dx).wait_send()
    for i, f in around:
        lr_send(i, f).wait_send()
    for i in (1, 2, 3):
        lr_send_y(i).wait_send()
    for i in range(1, 8):
        az_send(i).wait_send()
    a_far().wait_send()

    @pl.when(jnp.logical_not(home))
    def _():
        a_near().wait_send()

    for b in (0, 1):
        @pl.when(home & (c != b))
        def _():
            for m in range(3):
                w0_near(b, m).wait_send()
            ab_near(b).wait_send()

        @pl.when(jnp.logical_not(home))
        def _():
            for m in range(3):
                w0_far(b, m).wait_send()


def hand_on(lr_in, ig_in, abg_in, lr_out, ig_out, abg_out):
    lr_out[...] = lr_in[0]
    ig_out[...] = ig_in[...]
    abg_out[...] = abg_in[...]


def on_device(tokens, upstream, gate_weight, up_weight, down_weight, adapter_a, adapter_b, membership):
    vmem, dma = pltpu.VMEM, pltpu.SemaphoreType.DMA
    anywhere = pl.BlockSpec(memory_space=pl.ANY)
    inside = pl.BlockSpec(memory_space=pltpu.VMEM)
    log_ratio, input_grad, b_gradient = pl.pallas_call(
        kernel,
        out_shape=(
            jax.ShapeDtypeStruct((1, ROWS), F32),
            jax.ShapeDtypeStruct((BLK, ROWS), BF16),
            jax.ShapeDtypeStruct((8, 2 * COLS), F32),
        ),
        in_specs=[anywhere] * 7 + [inside],
        out_specs=(inside,) * 3,
        scratch_shapes=[
            vmem((2, 2, 4, 4, BLK, ROWS), BF16),
            vmem((16, BLK, W + 3 * COLS), BF16),
            vmem((2 * RANK, COLS), BF16),
            vmem((2, 1, ROWS), jnp.int32),
            vmem((W + 2 * COLS, 2 * ROWS), F32),
            vmem((COLS, 2 * ROWS), F32),
            vmem((W + 2 * COLS, 2 * ROWS), BF16),
            vmem((8, BLK, 2 * ROWS), BF16),
            vmem((8, BLK, 2 * ROWS), BF16),
            vmem((4, 4, BLK, ROWS), BF16),
            vmem((2, 2, CUT, ROWS), BF16),
            vmem((2, 2, 2, CUT, ROWS), BF16),
            vmem((4, BLK - CUT, ROWS), BF16),
            vmem((2, 4, BLK - CUT, ROWS), BF16),
            vmem((2, 2, 96, ROWS), BF16),
            vmem((2, 2, CUT, ROWS), BF16),
            vmem((1, 2 * ROWS), F32),
            vmem((4, 2, 1, 2 * ROWS), F32),
            vmem((4, 1, 2 * ROWS), F32),
            vmem((2, 1, ROWS), F32),
            vmem((8, 2, 8, COLS), F32),
            vmem((8, 2, 8, COLS), F32),
            vmem((2, 8, COLS), F32),
            vmem((2, 8, COLS), F32),
            dma((2, 4, 4, 2)),
            dma((2, 4, 4)),
            dma((2, 24)),
            dma((2, 4, 4)),
            dma((2,)),
            dma((2, 3)),
            dma((2, 3)),
            dma((16,)),
            dma((2, 16)),
            dma((1,)),
            dma((2,)),
            dma((2,)),
            dma((8,)),
            dma((8,)),
            dma((3, 2)),
            dma((3, 2)),
            dma((3, 4)),
            dma((3, 4)),
            dma((2, 2, 2)),
            dma((2, 2, 2)),
            dma((11,)),
            dma((11,)),
            dma((8,)),
            dma((8,)),
            dma((2,)),
            dma((2,)),
        ],
        compiler_params=pltpu.CompilerParams(
            collective_id=0, has_side_effects=True, vmem_limit_bytes=56 * 1024 * 1024
        ),
    )(
        tokens.T, upstream.T, gate_weight, up_weight, down_weight,
        adapter_a.reshape(16, BLK, 2 * RANK), adapter_b, membership.reshape(1, ROWS),
    )
    log_ratio, input_grad, b_gradient = pl.pallas_call(
        hand_on,
        out_shape=(
            jax.ShapeDtypeStruct((ROWS,), F32),
            jax.ShapeDtypeStruct((BLK, ROWS), BF16),
            jax.ShapeDtypeStruct((8, 2 * COLS), F32),
        ),
        in_specs=[inside] * 3,
        out_specs=(inside,) * 3,
    )(log_ratio, input_grad, b_gradient)
    return log_ratio, input_grad.T, b_gradient


def solution(mesh):
    placed = (
        P("dp", "tensor"),
        P("dp", "tensor"),
        P("dp", "tensor"),
        P("dp", "tensor"),
        P("dp", "tensor"),
        P(),
        P(None, "tensor"),
        P("dp"),
    )
    return jax.shard_map(
        on_device,
        mesh=mesh,
        in_specs=placed,
        out_specs=(P("dp"), P("dp", "tensor"), P("dp", "tensor")),
        check_vma=False,
    )
```

```python
import math

import jax
import jax.numpy as jnp
from jax import lax
from jax.experimental import pallas as pl
from jax.experimental.pallas import tpu as pltpu
from jax.sharding import PartitionSpec as P

MESH = pl.DeviceIdType.MESH
BF16 = jnp.bfloat16
F32 = jnp.float32

adapter_scale = 0.5
beta_coef = 0.5
loss_scale = 128.0

ROWS = 256
BLK = 320
COLS = 256
RANK = 64
W = 2 * RANK
D = 5120
CUT = 176


def tn(left, right):
    return lax.dot_general(left, right, (((0,), (0,)), ((), ())), preferred_element_type=F32)


def nt(left, right):
    return lax.dot_general(left, right, (((1,), (1,)), ((), ())), preferred_element_type=F32)


def dot(left, right):
    return jnp.dot(left, right, preferred_element_type=F32)


def m4(v):
    return lax.rem(v + 4, 4)


def m8(v):
    return lax.rem(v + 8, 8)


def kernel(
    tok, ups, wg, wu, wd, aa_in, ab_in, mem,
    lr_out, ig_out, abg_out,
    xb, wb, ab, mb, gu, rr, hc, sb, rb, pb,
    r1, r2, r3, r4, r5, r6, lr_own, lrx, lry, cf, apart, azb, afin, abr,
    xr, xd, xs, xds, xl, w0r, w0s, zr, zs, aas, abs_, mrs, d2s, d2r, rar, ras, rbr, rbs, rcr, rcs, lrr, lrs, azr, azs, afr, afs,
):
    dp = lax.axis_index("dp")
    tp = lax.axis_index("tensor")
    yl, z = lax.div(dp, 8), lax.rem(dp, 8)
    x, yh, c = lax.div(tp, 4), lax.rem(lax.div(tp, 2), 2), lax.rem(tp, 2)
    y = yh * 2 + yl

    def dev(x_, y_, z_, c_):
        return {"dp": lax.rem(y_, 2) * 8 + z_, "tensor": x_ * 4 + lax.div(y_, 2) * 2 + c_}

    def copy(src, dst, ssem, rsem, to):
        return pltpu.make_async_remote_copy(
            src_ref=src, dst_ref=dst, send_sem=ssem, recv_sem=rsem, device_id=to, device_id_type=MESH
        )

    sib = dev(x, y, z, 1 - c)
    other_y = yh * 2 + (1 - yl)
    pending = []

    def send(*args):
        descriptor = copy(*args)
        descriptor.start()
        pending.append(descriptor)

    def got(dst, rsem):
        copy(dst, dst, rsem, rsem, sib).wait_recv()

    barrier = pltpu.get_barrier_semaphore()
    partners = [sib, dev(x, other_y, z, 1 - c)]
    partners += [dev(m4(x + i), y, z, c) for i in (1, 2, 3)]
    partners += [dev(m4(x + i), y, z, 1 - c) for i in (1, 2, 3)]
    partners += [dev(x, m4(y + i), z, c) for i in (1, 2, 3)]
    partners += [dev(x, y, m8(z + i), c) for i in range(1, 8)]
    for partner in partners:
        pl.semaphore_signal(barrier, inc=1, device_id=partner, device_id_type=MESH)
    pl.semaphore_wait(barrier, len(partners))

    kf, ks = yl * 8 + z, (1 - yl) * 8 + z
    home = c == yl
    mats = (wg, wu, wd)

    def w0(b, m):
        return mats[m].at[:, b * COLS:(b + 1) * COLS], wb.at[kf, :, W + m * COLS:W + (m + 1) * COLS]

    def w0_local(b, m):
        return pltpu.make_async_copy(*w0(b, m), w0r.at[0, m])

    def w0_near(b, m):
        return copy(*w0(b, m), w0s.at[b, m], w0r.at[0, m], sib)

    def w0_far(b, m):
        return copy(*w0(b, m), w0s.at[b, m], w0r.at[1, m], dev(x, yh * 2 + c, z, b))

    def ab_local(b):
        return pltpu.make_async_copy(ab_in.at[:, b * COLS:(b + 1) * COLS], ab, abs_.at[0])

    def ab_near(b):
        return copy(ab_in.at[:, b * COLS:(b + 1) * COLS], ab, abs_.at[1], abs_.at[0], sib)

    for b in (0, 1):
        @pl.when(home & (c == b))
        def _():
            for m in range(3):
                w0_local(b, m).start()

        @pl.when(home & (c != b))
        def _():
            for m in range(3):
                w0_near(b, m).start()

    sources = (tok, ups)

    def place(t, i, j):
        return (m4(x + i), m4(y + j)) if t == 0 else (m4(x + j), m4(y + i))

    def slot(t, i, j, rows=slice(0, BLK), core=None):
        px, py = place(t, i, j)
        return xb.at[t, c if core is None else core, px, py, rows]

    def to(t, i, j):
        px, py = place(t, i, j)
        return dev(px, py, z, c)

    halves = (slice(0, BLK // 2), slice(BLK // 2, BLK))
    counts = [0, 0]

    def xsend(t, src, dst, i, j, key):
        n = counts[t]
        counts[t] += 1
        send(src, dst, xs.at[t, n], xr.at[(t,) + key], to(t, i, j))

    def share(t, i, j, src=None):
        send(slot(t, i, j) if src is None else src, slot(t, i, j), xds.at[t, i, j], xd.at[t, i, j], sib)

    own_local = [pltpu.make_async_copy(sources[t], slot(t, 0, 0), xl.at[t]) for t in (0, 1)]
    for t in (0, 1):
        own_local[t].start()
    for t in (0, 1):
        xsend(t, sources[t], slot(t, 0, 0), 1, 0, (3, 0, 0))
        xsend(t, sources[t], slot(t, 0, 0), -1, 0, (1, 0, 0))

    for b in (0, 1):
        @pl.when(jnp.logical_not(home))
        def _():
            for m in range(3):
                w0_far(b, m).start()

        @pl.when(home & (c == b))
        def _():
            ab_local(b).start()

        @pl.when(home & (c != b))
        def _():
            ab_near(b).start()

    aa_copy = pltpu.make_async_copy(aa_in, wb.at[:, :, 0:W], aas.at[0])
    aa_copy.start()
    send(mem, mb.at[yl], mrs.at[0], mrs.at[1], dev(x, other_y, z, c))
    mb[yl] = mem[...]

    def weights(ref, k):
        return ref.at[k, :, W:W + 3 * COLS]

    def w0_wait(first, k):
        for m in range(3):
            ref = wb.at[k, :, W + m * COLS:W + (m + 1) * COLS]
            if first:
                @pl.when(home)
                def _():
                    pltpu.make_async_copy(ref, ref, w0r.at[0, m]).wait()

                @pl.when(jnp.logical_not(home))
                def _():
                    got(ref, w0r.at[0, m])
            else:
                got(ref, w0r.at[1, m])

    up_z, down_z = dev(x, y, m8(z + 1), c), dev(x, y, m8(z - 1), c)

    w0_wait(True, kf)
    send(weights(wb, kf), weights(wb, kf), zs.at[0, 0], zr.at[2], up_z)
    send(weights(wb, kf), weights(wb, kf), zs.at[1, 0], zr.at[3], down_z)

    for t in (0, 1):
        xsend(t, sources[t], slot(t, 0, 0), 0, 1, (0, 3, 0))
        xsend(t, sources[t], slot(t, 0, 0), 0, -1, (0, 1, 0))
        share(t, 0, 0, sources[t])

    def across(t, i):
        xsend(t, slot(t, i, 0), slot(t, i, 0), 0, 1, (i % 4, 3, 0))
        xsend(t, slot(t, i, 0), slot(t, i, 0), 0, -1, (i % 4, 1, 0))
        share(t, i, 0)

    for t in (0, 1):
        for i, step, half in ((3, 1, 0), (1, -1, 1)):
            got(slot(t, i, 0), xr.at[t, i, 0, 0])
            xsend(t, slot(t, i, 0, halves[half]), slot(t, i, 0, halves[half]), step, 0, (2, 0, half))
    for t in (0, 1):
        across(t, 3)
        across(t, 1)

    w0_wait(False, ks)
    send(weights(wb, ks), weights(wb, ks), zs.at[0, 1], zr.at[4], up_z)
    send(weights(wb, ks), weights(wb, ks), zs.at[1, 1], zr.at[5], down_z)

    for t in (0, 1):
        for half in (0, 1):
            got(slot(t, 2, 0, halves[half]), xr.at[t, 2, 0, half])
        across(t, 2)

    def block_of(i):
        j = i - 2
        distance = lax.div(j, 4) + 1
        kind = lax.rem(j, 4)
        down = lax.rem(kind, 2)
        second = jnp.where(i == 15, 1, lax.div(kind, 2))
        zz = m8(z + jnp.where(down == 1, distance, -distance))
        zz = jnp.where(i < 2, z, zz)
        second = jnp.where(i < 2, i, second)
        return jnp.where(second == 1, 1 - yl, yl) * 8 + zz

    def zcopy(i, down, later):
        k = block_of(jnp.int32(i))
        return copy(weights(wb, k), weights(wb, k), zs.at[down, i], zr.at[later], down_z if down else up_z)

    def zstep(i):
        got(weights(wb, block_of(jnp.int32(i))), zr.at[i])
        down = (i - 2) % 2
        later = i + 4 if i <= 10 else 15
        if i <= 10 or i == 13:
            send(*[weights(wb, block_of(jnp.int32(i)))] * 2, zs.at[down, i], zr.at[later], down_z if down else up_z)

    for i in (2, 3):
        zstep(i)

    def pass_on(t, i):
        got(slot(t, i, 3), xr.at[t, i, 3, 0])
        xsend(t, slot(t, i, 3, halves[0]), slot(t, i, 3, halves[0]), 0, 1, (i, 2, 0))
        share(t, i, 3)
        got(slot(t, i, 1), xr.at[t, i, 1, 0])
        xsend(t, slot(t, i, 1, halves[1]), slot(t, i, 1, halves[1]), 0, -1, (i, 2, 1))
        share(t, i, 1)

    for i in (0, 3, 1):
        for t in (0, 1):
            pass_on(t, i)
    for i in (4, 5):
        zstep(i)
    for t in (0, 1):
        pass_on(t, 2)
    for i in (6, 7):
        zstep(i)
    for i in (0, 3, 1, 2):
        for t in (0, 1):
            for half in (0, 1):
                got(slot(t, i, 2, halves[half]), xr.at[t, i, 2, half])
            share(t, i, 2)
    for t in (0, 1):
        own_local[t].wait()
        for i in range(4):
            for j in range(4):
                got(slot(t, i, j, core=1 - c), xd.at[t, i, j])
    aa_copy.wait()

    gu[...] = jnp.zeros_like(gu)
    rr[...] = jnp.zeros_like(rr)

    def forward(i, carry):
        for e in range(8, 16):
            @pl.when(i == e)
            def _():
                got(weights(wb, block_of(jnp.int32(e))), zr.at[e])
                if e <= 10 or e == 13:
                    zcopy(e, (e - 2) % 2, e + 4 if e <= 10 else 15).start()

        k = block_of(i)
        kx, ky, kc = lax.div(k, 4), lax.rem(lax.div(k, 2), 2) * 2, lax.rem(k, 2)
        t = jnp.concatenate([xb[0, kc, kx, ky], xb[0, kc, kx, ky + 1]], axis=1)
        u = jnp.concatenate([xb[1, kc, kx, ky], xb[1, kc, kx, ky + 1]], axis=1)
        gu[...] += tn(wb[k, :, 0:W + 2 * COLS], t)
        rr[...] += tn(wb[k, :, W + 2 * COLS:W + 3 * COLS], u)
        return carry

    lax.fori_loop(0, 16, forward, 0)

    @pl.when(home)
    def _():
        pltpu.make_async_copy(ab, ab, abs_.at[0]).wait()

    @pl.when(jnp.logical_not(home))
    def _():
        got(ab, abs_.at[0])

    low = gu[0:W].astype(BF16)
    b_t = ab[...].astype(F32).T.astype(BF16)
    step = 64
    ratio = jnp.zeros((1, 2 * ROWS), F32)
    for r in range(COLS // step):
        units = slice(r * step, (r + 1) * step)
        g_at, u_at = W + r * step, W + COLS + r * step
        gate, up, readout = gu[g_at:g_at + step], gu[u_at:u_at + step], rr[units]
        pol_gate = gate + adapter_scale * dot(b_t[units, 0:RANK], low[0:RANK])
        pol_up = up + adapter_scale * dot(b_t[units, RANK:W], low[RANK:W])
        sig = jax.nn.sigmoid(pol_gate)
        act = pol_gate * sig
        shift = act * pol_up - gate * jax.nn.sigmoid(gate) * up
        ratio += jnp.sum(shift * readout, axis=0, keepdims=True)
        scaled = readout * (1.0 / math.sqrt(D))
        hc[g_at:g_at + step] = (scaled * pol_up * (sig * (1.0 + pol_gate * (1.0 - sig)))).astype(BF16)
        hc[u_at:u_at + step] = (scaled * act).astype(BF16)
    lr_own[...] = ratio
    lrx[x, c] = ratio
    around = [(i, f) for i in range(4) for f in (0, 1) if i or f]

    def lr_send(i, f):
        n, core = 2 * i + f, 1 - c if f else c
        return copy(lr_own, lrx.at[x, c], lrs.at[n], lrr.at[n], dev(m4(x + i), y, z, core))

    def lr_send_y(i):
        return copy(lry.at[y], lry.at[y], lrs.at[7 + i], lrr.at[7 + i], dev(x, m4(y + i), z, c))

    for i, f in around:
        lr_send(i, f).start()
    hc[0:RANK] = (adapter_scale * dot(ab[0:RANK], hc[W:W + COLS])).astype(BF16)
    hc[RANK:W] = (adapter_scale * dot(ab[RANK:W], hc[W + COLS:])).astype(BF16)

    first, second = slice(0, CUT), slice(CUT, BLK)

    def order(j):
        turn = lax.rem(j + 1, 3)
        dx = jnp.where(j < 2, 2, jnp.where(turn == 0, 1, jnp.where(turn == 1, 3, 0)))
        dh = jnp.where(j < 2, 1 - j, jnp.where(j < 5, 1, 0))
        return lax.rem(x + dx, 4), lax.rem(yh + dh, 2)

    def product(j, core):
        bx, bh = order(j)
        return dot(wb[bx * 4 + bh * 2 + core, :, 0:W + 2 * COLS], hc[...])

    def to_sib(j):
        return copy(sb.at[j], rb.at[j], d2s.at[j], d2r.at[j], sib)

    def back_send(j):
        sb[j] = product(j, 1 - c).astype(BF16)
        to_sib(j).start()

    up_x, down_x = dev(m4(x + 1), y, z, c), dev(m4(x - 1), y, z, c)
    up_y, down_y = dev(x, m4(y + 1), z, c), dev(x, m4(y - 1), z, c)
    far, near = (1 - yh) * 2, yh * 2
    pairs = (pl.ds(far, 2), pl.ds(near, 2))

    def fold(idx, ref):
        pb[idx] = (pb[idx].astype(F32) + ref[...].astype(F32)).astype(BF16)

    def a1(d):
        return copy(pb.at[m4(x + 2), pairs[d], first], r1.at[d], ras.at[0, d], rar.at[0, d], (up_x, down_x)[d])

    def a2(d, n):
        return copy(
            pb.at[m4(x + 1 - 2 * d), pairs[n], first], r2.at[d, n], ras.at[1 + n, d], rar.at[1 + n, d], (up_x, down_x)[d]
        )

    def a_fold(d):
        got(r1.at[d], rar.at[0, d])
        fold((m4(x + 1 - 2 * d), pairs[d], first), r1.at[d])

    def b_dir(dx):
        return 0 if dx in (1, 2) else 1

    def b1(dx):
        d = b_dir(dx)
        return copy(pb.at[m4(x + dx), m4(y + 2), second], r3.at[dx], rbs.at[0, dx], rbr.at[0, dx], (up_y, down_y)[d])

    def b2(dx, d):
        return copy(
            pb.at[m4(x + dx), m4(y + 1 - 2 * d), second], r4.at[d, dx], rbs.at[1 + d, dx], rbr.at[1 + d, dx], (up_y, down_y)[d]
        )

    def b_fold(dx):
        got(r3.at[dx], rbr.at[0, dx])
        fold((m4(x + dx), m4(y + 1 - 2 * b_dir(dx)), second), r3.at[dx])

    def b_both(dx):
        b_fold(dx)
        b2(dx, 0).start()
        b2(dx, 1).start()

    def after(j):
        if j == 0:
            a1(0).start()
            b1(2).start()
        elif j == 1:
            a1(1).start()
        elif j == 2:
            b1(1).start()
        elif j == 3:
            b1(3).start()
            a2(1, 0).start()
        elif j == 4:
            b1(0).start()
            a_fold(0)
            a2(0, 0).start()
            b_both(2)
        elif j == 5:
            a2(0, 1).start()
            b_both(1)
        elif j == 6:
            a_fold(1)
            a2(1, 1).start()
            b_both(3)
        else:
            b_both(0)

    def az_send(i):
        return copy(apart.at[m8(z + i)], azb.at[z], azs.at[i], azr.at[i], dev(x, y, m8(z + i), c))

    def coefficients():
        for i in (1, 2, 3):
            got(lry.at[m4(y - i)], lrr.at[7 + i])
        lr_row = (((lry[0] + lry[1]) + lry[2]) + lry[3]) / math.sqrt(D)
        got(mb.at[1 - yl], mrs.at[1])
        eye2 = lax.broadcasted_iota(jnp.int32, (ROWS, ROWS), 0) == lax.broadcasted_iota(jnp.int32, (ROWS, ROWS), 1)

        def column(row):
            return jnp.sum(jnp.where(eye2, row, 0.0), axis=1, keepdims=True)

        for g in (0, 1):
            members = mb[g]
            pair = lax.shift_right_logical(members, 1)
            side = (1 - 2 * (members - 2 * pair)).astype(F32)
            pair = pair.astype(F32)
            lr_g = lr_row[:, g * ROWS:(g + 1) * ROWS]
            growth = jnp.exp(lr_g)
            same = column(pair) == pair
            margin = beta_coef * jnp.sum(jnp.where(same, column(side * (growth + lr_g)), 0.0), axis=0, keepdims=True)
            cf[g] = -loss_scale * beta_coef * jax.nn.sigmoid(-margin) * side * (growth + 1.0)

            @pl.when(yl == g)
            def _():
                lr_out[...] = lr_g

        low_t = (gu[0:W].astype(BF16).astype(F32) * jnp.concatenate([cf[0], cf[1]], axis=1)).astype(BF16)
        g_part = adapter_scale * nt(low_t[0:RANK], hc[W:W + COLS])
        u_part = adapter_scale * nt(low_t[RANK:W], hc[W + COLS:])
        apart[:, 0] = g_part.reshape(8, 8, COLS)
        apart[:, 1] = u_part.reshape(8, 8, COLS)
        for i in range(1, 8):
            az_send(i).start()
        azb[z] = apart[z]

    def a_near():
        return copy(afin.at[yl], abr.at[c], afs.at[0], afr.at[c], sib)

    def a_far():
        return copy(afin.at[1 - yl], abr.at[c], afs.at[1], afr.at[c], dev(x, other_y, z, yl))

    def hand_out():
        for i in range(1, 8):
            got(azb.at[m8(z - i)], azr.at[i])
        total = azb[0]
        for i in range(1, 8):
            total = total + azb[i]
        afin[...] = total

        a_far().start()

        @pl.when(home)
        def _():
            abr[c] = afin[yl]

        @pl.when(jnp.logical_not(home))
        def _():
            a_near().start()

    def log_ratios():
        for i, f in around:
            got(lrx.at[m4(x - i), 1 - c if f else c], lrr.at[2 * i + f])
        rows = [lrx[i, 0] + lrx[i, 1] for i in range(4)]
        lry[y] = ((rows[0] + rows[1]) + rows[2]) + rows[3]
        for i in (1, 2, 3):
            lr_send_y(i).start()

    back_send(0)

    def backward(j, carry):
        @pl.when(j < 7)
        def _():
            back_send(j + 1)

        total = product(j, c)
        to_sib(j).wait_recv()
        bx, bh = order(j)
        total = (total + rb[j].astype(F32)).astype(BF16)
        pb[bx, bh * 2] = total[:, 0:ROWS]
        pb[bx, bh * 2 + 1] = total[:, ROWS:]
        for e in range(8):
            @pl.when(j == e)
            def _():
                after(e)
                if e == 1:
                    log_ratios()
                if e == 5:
                    coefficients()
        return carry

    lax.fori_loop(0, 8, backward, 0)

    quarter = ((slice(0, 96), slice(96, CUT)), (slice(CUT, 256), slice(256, BLK)))
    size = ((96, CUT - 96), (256 - CUT, BLK - 256))
    span = (CUT, BLK - CUT)

    def near_of(h, i):
        return (x, m4(y + i)) if h == 0 else (m4(x + i), y)

    ways = ((up_y, down_y), (up_x, down_x))

    def c1(h, d):
        return copy(pb.at[near_of(h, 2) + (quarter[h][d],)], r5.at[h, d, 0:size[h][d]], rcs.at[0, h, d], rcr.at[0, h, d], ways[h][d])

    def c2(h, d):
        rows = (first, second)[h]
        return copy(pb.at[near_of(h, 1 - 2 * d) + (rows,)], r6.at[h, d, 0:span[h]], rcs.at[1, h, d], rcr.at[1, h, d], ways[h][d])

    def x_sum(n):
        for d in (0, 1):
            got(r2.at[d, n], rar.at[1 + n, d])
        idx = (x, pairs[n], first)
        pb[idx] = (pb[idx].astype(F32) + r2[0, n].astype(F32) + r2[1, n].astype(F32)).astype(BF16)

    def y_sum(i):
        for d in (0, 1):
            got(r4.at[d, i], rbr.at[1 + d, i])
        idx = (m4(x + i), y, second)
        pb[idx] = (pb[idx].astype(F32) + r4[0, i].astype(F32) + r4[1, i].astype(F32)).astype(BF16)

    def second_hop(h):
        for d in (0, 1):
            got(r5.at[h, d, 0:size[h][d]], rcr.at[0, h, d])
            fold(near_of(h, 1 - 2 * d) + (quarter[h][d],), r5.at[h, d, 0:size[h][d]])
            c2(h, d).start()

    x_sum(0)
    for d in (0, 1):
        c1(0, d).start()
    y_sum(2)
    for d in (0, 1):
        c1(1, d).start()
    x_sum(1)
    y_sum(1)
    second_hop(0)
    y_sum(3)
    second_hop(1)
    y_sum(0)
    hand_out()

    for h in (0, 1):
        for d in (0, 1):
            got(r6.at[h, d, 0:span[h]], rcr.at[1, h, d])
        rows = (first, second)[h]
        grad = pb[x, y, rows].astype(F32) + r6[h, 0, 0:span[h]].astype(F32) + r6[h, 1, 0:span[h]].astype(F32)
        ig_out[rows, :] = (grad * cf[yl]).astype(BF16)

    @pl.when(home)
    def _():
        got(abr.at[1 - c], afr.at[1 - c])

    @pl.when(jnp.logical_not(home))
    def _():
        got(abr.at[0], afr.at[0])
        got(abr.at[1], afr.at[1])

    abg_out[:, 0:COLS] = abr[0]
    abg_out[:, COLS:2 * COLS] = abr[1]

    for descriptor in pending:
        descriptor.wait_send()
    for e in (8, 9, 10, 13):
        zcopy(e, (e - 2) % 2, e + 4 if e <= 10 else 15).wait_send()

    def sent(j, carry):
        to_sib(j).wait_send()
        return carry

    lax.fori_loop(0, 8, sent, 0)
    for d in (0, 1):
        a1(d).wait_send()
        for n in (0, 1):
            a2(d, n).wait_send()
        for dx in range(4):
            b2(dx, d).wait_send()
        for h in (0, 1):
            c1(h, d).wait_send()
            c2(h, d).wait_send()
    for dx in range(4):
        b1(dx).wait_send()
    for i, f in around:
        lr_send(i, f).wait_send()
    for i in (1, 2, 3):
        lr_send_y(i).wait_send()
    for i in range(1, 8):
        az_send(i).wait_send()
    a_far().wait_send()

    @pl.when(jnp.logical_not(home))
    def _():
        a_near().wait_send()

    for b in (0, 1):
        @pl.when(home & (c != b))
        def _():
            for m in range(3):
                w0_near(b, m).wait_send()
            ab_near(b).wait_send()

        @pl.when(jnp.logical_not(home))
        def _():
            for m in range(3):
                w0_far(b, m).wait_send()


def hand_on(lr_in, ig_in, abg_in, lr_out, ig_out, abg_out):
    lr_out[...] = lr_in[0]
    ig_out[...] = ig_in[...]
    abg_out[...] = abg_in[...]


def on_device(tokens, upstream, gate_weight, up_weight, down_weight, adapter_a, adapter_b, membership):
    vmem, dma = pltpu.VMEM, pltpu.SemaphoreType.DMA
    anywhere = pl.BlockSpec(memory_space=pl.ANY)
    inside = pl.BlockSpec(memory_space=pltpu.VMEM)
    log_ratio, input_grad, b_gradient = pl.pallas_call(
        kernel,
        out_shape=(
            jax.ShapeDtypeStruct((1, ROWS), F32),
            jax.ShapeDtypeStruct((BLK, ROWS), BF16),
            jax.ShapeDtypeStruct((8, 2 * COLS), F32),
        ),
        in_specs=[anywhere] * 7 + [inside],
        out_specs=(inside,) * 3,
        scratch_shapes=[
            vmem((2, 2, 4, 4, BLK, ROWS), BF16),
            vmem((16, BLK, W + 3 * COLS), BF16),
            vmem((2 * RANK, COLS), BF16),
            vmem((2, 1, ROWS), jnp.int32),
            vmem((W + 2 * COLS, 2 * ROWS), F32),
            vmem((COLS, 2 * ROWS), F32),
            vmem((W + 2 * COLS, 2 * ROWS), BF16),
            vmem((8, BLK, 2 * ROWS), BF16),
            vmem((8, BLK, 2 * ROWS), BF16),
            vmem((4, 4, BLK, ROWS), BF16),
            vmem((2, 2, CUT, ROWS), BF16),
            vmem((2, 2, 2, CUT, ROWS), BF16),
            vmem((4, BLK - CUT, ROWS), BF16),
            vmem((2, 4, BLK - CUT, ROWS), BF16),
            vmem((2, 2, 96, ROWS), BF16),
            vmem((2, 2, CUT, ROWS), BF16),
            vmem((1, 2 * ROWS), F32),
            vmem((4, 2, 1, 2 * ROWS), F32),
            vmem((4, 1, 2 * ROWS), F32),
            vmem((2, 1, ROWS), F32),
            vmem((8, 2, 8, COLS), F32),
            vmem((8, 2, 8, COLS), F32),
            vmem((2, 8, COLS), F32),
            vmem((2, 8, COLS), F32),
            dma((2, 4, 4, 2)),
            dma((2, 4, 4)),
            dma((2, 24)),
            dma((2, 4, 4)),
            dma((2,)),
            dma((2, 3)),
            dma((2, 3)),
            dma((16,)),
            dma((2, 16)),
            dma((1,)),
            dma((2,)),
            dma((2,)),
            dma((8,)),
            dma((8,)),
            dma((3, 2)),
            dma((3, 2)),
            dma((3, 4)),
            dma((3, 4)),
            dma((2, 2, 2)),
            dma((2, 2, 2)),
            dma((11,)),
            dma((11,)),
            dma((8,)),
            dma((8,)),
            dma((2,)),
            dma((2,)),
        ],
        compiler_params=pltpu.CompilerParams(
            collective_id=0, has_side_effects=True, vmem_limit_bytes=56 * 1024 * 1024
        ),
    )(
        tokens.T, upstream.T, gate_weight, up_weight, down_weight,
        adapter_a.reshape(16, BLK, 2 * RANK), adapter_b, membership.reshape(1, ROWS),
    )
    log_ratio, input_grad, b_gradient = pl.pallas_call(
        hand_on,
        out_shape=(
            jax.ShapeDtypeStruct((ROWS,), F32),
            jax.ShapeDtypeStruct((BLK, ROWS), BF16),
            jax.ShapeDtypeStruct((8, 2 * COLS), F32),
        ),
        in_specs=[inside] * 3,
        out_specs=(inside,) * 3,
    )(log_ratio, input_grad, b_gradient)
    return log_ratio, input_grad.T, b_gradient


def solution(mesh):
    placed = (
        P("dp", "tensor"),
        P("dp", "tensor"),
        P("dp", "tensor"),
        P("dp", "tensor"),
        P("dp", "tensor"),
        P(),
        P(None, "tensor"),
        P("dp"),
    )
    return jax.shard_map(
        on_device,
        mesh=mesh,
        in_specs=placed,
        out_specs=(P("dp"), P("dp", "tensor"), P("dp", "tensor")),
        check_vma=False,
    )
```

```python
import math

import jax
import jax.numpy as jnp
from jax import lax
from jax.experimental import pallas as pl
from jax.experimental.pallas import tpu as pltpu
from jax.sharding import PartitionSpec as P

MESH = pl.DeviceIdType.MESH
BF16 = jnp.bfloat16
F32 = jnp.float32

adapter_scale = 0.5
beta_coef = 0.5
loss_scale = 128.0

ROWS = 256
BLK = 320
COLS = 256
RANK = 64
W = 2 * RANK
D = 5120
CUT = 176


def tn(left, right):
    return lax.dot_general(left, right, (((0,), (0,)), ((), ())), preferred_element_type=F32)


def nt(left, right):
    return lax.dot_general(left, right, (((1,), (1,)), ((), ())), preferred_element_type=F32)


def dot(left, right):
    return jnp.dot(left, right, preferred_element_type=F32)


def m4(v):
    return lax.rem(v + 4, 4)


def m8(v):
    return lax.rem(v + 8, 8)


def kernel(
    tok, ups, wg, wu, wd, aa_in, ab_in, mem,
    lr_out, ig_out, abg_out,
    xb, wb, ab, mb, gu, rr, hc, sb, rb, pb,
    r1, r2, r3, r4, r5, r6, lr_own, lrx, lry, cf, apart, azb, afin, abr,
    xr, xd, xs, xds, xl, w0r, w0s, zr, zs, aas, abs_, mrs, d2s, d2r, rar, ras, rbr, rbs, rcr, rcs, lrr, lrs, azr, azs, afr, afs,
):
    dp = lax.axis_index("dp")
    tp = lax.axis_index("tensor")
    yl, z = lax.div(dp, 8), lax.rem(dp, 8)
    x, yh, c = lax.div(tp, 4), lax.rem(lax.div(tp, 2), 2), lax.rem(tp, 2)
    y = yh * 2 + yl

    def dev(x_, y_, z_, c_):
        return {"dp": lax.rem(y_, 2) * 8 + z_, "tensor": x_ * 4 + lax.div(y_, 2) * 2 + c_}

    def copy(src, dst, ssem, rsem, to):
        return pltpu.make_async_remote_copy(
            src_ref=src, dst_ref=dst, send_sem=ssem, recv_sem=rsem, device_id=to, device_id_type=MESH
        )

    sib = dev(x, y, z, 1 - c)
    other_y = yh * 2 + (1 - yl)
    pending = []

    def send(*args):
        descriptor = copy(*args)
        descriptor.start()
        pending.append(descriptor)

    def got(dst, rsem):
        copy(dst, dst, rsem, rsem, sib).wait_recv()

    barrier = pltpu.get_barrier_semaphore()
    partners = [sib, dev(x, other_y, z, 1 - c)]
    partners += [dev(m4(x + i), y, z, c) for i in (1, 2, 3)]
    partners += [dev(m4(x + i), y, z, 1 - c) for i in (1, 2, 3)]
    partners += [dev(x, m4(y + i), z, c) for i in (1, 2, 3)]
    partners += [dev(x, y, m8(z + i), c) for i in range(1, 8)]
    for partner in partners:
        pl.semaphore_signal(barrier, inc=1, device_id=partner, device_id_type=MESH)
    pl.semaphore_wait(barrier, len(partners))

    kf, ks = yl * 8 + z, (1 - yl) * 8 + z
    home = c == yl
    mats = (wg, wu, wd)

    def w0(b, m):
        return mats[m].at[:, b * COLS:(b + 1) * COLS], wb.at[kf, :, W + m * COLS:W + (m + 1) * COLS]

    def w0_local(b, m):
        return pltpu.make_async_copy(*w0(b, m), w0r.at[0, m])

    def w0_near(b, m):
        return copy(*w0(b, m), w0s.at[b, m], w0r.at[0, m], sib)

    def w0_far(b, m):
        return copy(*w0(b, m), w0s.at[b, m], w0r.at[1, m], dev(x, yh * 2 + c, z, b))

    def ab_local(b):
        return pltpu.make_async_copy(ab_in.at[:, b * COLS:(b + 1) * COLS], ab, abs_.at[0])

    def ab_near(b):
        return copy(ab_in.at[:, b * COLS:(b + 1) * COLS], ab, abs_.at[1], abs_.at[0], sib)

    for b in (0, 1):
        @pl.when(home & (c == b))
        def _():
            for m in range(3):
                w0_local(b, m).start()

        @pl.when(home & (c != b))
        def _():
            for m in range(3):
                w0_near(b, m).start()

    sources = (tok, ups)

    def place(t, i, j):
        return (m4(x + i), m4(y + j)) if t == 0 else (m4(x + j), m4(y + i))

    def slot(t, i, j, rows=slice(0, BLK), core=None):
        px, py = place(t, i, j)
        return xb.at[t, c if core is None else core, px, py, rows]

    def to(t, i, j):
        px, py = place(t, i, j)
        return dev(px, py, z, c)

    halves = (slice(0, BLK // 2), slice(BLK // 2, BLK))
    counts = [0, 0]

    def xsend(t, src, dst, i, j, key):
        n = counts[t]
        counts[t] += 1
        send(src, dst, xs.at[t, n], xr.at[(t,) + key], to(t, i, j))

    def share(t, i, j, src=None):
        send(slot(t, i, j) if src is None else src, slot(t, i, j), xds.at[t, i, j], xd.at[t, i, j], sib)

    own_local = [pltpu.make_async_copy(sources[t], slot(t, 0, 0), xl.at[t]) for t in (0, 1)]
    for t in (0, 1):
        own_local[t].start()
    for t in (0, 1):
        xsend(t, sources[t], slot(t, 0, 0), 1, 0, (3, 0, 0))
        xsend(t, sources[t], slot(t, 0, 0), -1, 0, (1, 0, 0))

    for b in (0, 1):
        @pl.when(jnp.logical_not(home))
        def _():
            for m in range(3):
                w0_far(b, m).start()

        @pl.when(home & (c == b))
        def _():
            ab_local(b).start()

        @pl.when(home & (c != b))
        def _():
            ab_near(b).start()

    aa_copy = pltpu.make_async_copy(aa_in, wb.at[:, :, 0:W], aas.at[0])
    aa_copy.start()
    send(mem, mb.at[yl], mrs.at[0], mrs.at[1], dev(x, other_y, z, c))
    mb[yl] = mem[...]

    def weights(ref, k):
        return ref.at[k, :, W:W + 3 * COLS]

    def w0_wait(first, k):
        for m in range(3):
            ref = wb.at[k, :, W + m * COLS:W + (m + 1) * COLS]
            if first:
                @pl.when(home)
                def _():
                    pltpu.make_async_copy(ref, ref, w0r.at[0, m]).wait()

                @pl.when(jnp.logical_not(home))
                def _():
                    got(ref, w0r.at[0, m])
            else:
                got(ref, w0r.at[1, m])

    up_z, down_z = dev(x, y, m8(z + 1), c), dev(x, y, m8(z - 1), c)

    w0_wait(True, kf)
    send(weights(wb, kf), weights(wb, kf), zs.at[0, 0], zr.at[2], up_z)
    send(weights(wb, kf), weights(wb, kf), zs.at[1, 0], zr.at[3], down_z)

    for t in (0, 1):
        xsend(t, sources[t], slot(t, 0, 0), 0, 1, (0, 3, 0))
        xsend(t, sources[t], slot(t, 0, 0), 0, -1, (0, 1, 0))
        share(t, 0, 0, sources[t])

    def across(t, i):
        xsend(t, slot(t, i, 0), slot(t, i, 0), 0, 1, (i % 4, 3, 0))
        xsend(t, slot(t, i, 0), slot(t, i, 0), 0, -1, (i % 4, 1, 0))
        share(t, i, 0)

    for t in (0, 1):
        for i, step, half in ((3, 1, 0), (1, -1, 1)):
            got(slot(t, i, 0), xr.at[t, i, 0, 0])
            xsend(t, slot(t, i, 0, halves[half]), slot(t, i, 0, halves[half]), step, 0, (2, 0, half))
    for t in (0, 1):
        across(t, 3)
        across(t, 1)

    w0_wait(False, ks)
    send(weights(wb, ks), weights(wb, ks), zs.at[0, 1], zr.at[4], up_z)
    send(weights(wb, ks), weights(wb, ks), zs.at[1, 1], zr.at[5], down_z)

    for t in (0, 1):
        for half in (0, 1):
            got(slot(t, 2, 0, halves[half]), xr.at[t, 2, 0, half])
        across(t, 2)

    def block_of(i):
        j = i - 2
        distance = lax.div(j, 4) + 1
        kind = lax.rem(j, 4)
        down = lax.rem(kind, 2)
        second = jnp.where(i == 15, 1, lax.div(kind, 2))
        zz = m8(z + jnp.where(down == 1, distance, -distance))
        zz = jnp.where(i < 2, z, zz)
        second = jnp.where(i < 2, i, second)
        return jnp.where(second == 1, 1 - yl, yl) * 8 + zz

    def zcopy(i, down, later):
        k = block_of(jnp.int32(i))
        return copy(weights(wb, k), weights(wb, k), zs.at[down, i], zr.at[later], down_z if down else up_z)

    def zstep(i):
        got(weights(wb, block_of(jnp.int32(i))), zr.at[i])
        down = (i - 2) % 2
        later = i + 4 if i <= 10 else 15
        if i <= 10 or i == 13:
            send(*[weights(wb, block_of(jnp.int32(i)))] * 2, zs.at[down, i], zr.at[later], down_z if down else up_z)

    for i in (2, 3):
        zstep(i)

    def pass_on(t, i):
        got(slot(t, i, 3), xr.at[t, i, 3, 0])
        xsend(t, slot(t, i, 3, halves[0]), slot(t, i, 3, halves[0]), 0, 1, (i, 2, 0))
        share(t, i, 3)
        got(slot(t, i, 1), xr.at[t, i, 1, 0])
        xsend(t, slot(t, i, 1, halves[1]), slot(t, i, 1, halves[1]), 0, -1, (i, 2, 1))
        share(t, i, 1)

    for i in (0, 3, 1):
        for t in (0, 1):
            pass_on(t, i)
    for i in (4, 5):
        zstep(i)
    for t in (0, 1):
        pass_on(t, 2)
    for i in (6, 7):
        zstep(i)
    for i in (0, 3, 1, 2):
        for t in (0, 1):
            for half in (0, 1):
                got(slot(t, i, 2, halves[half]), xr.at[t, i, 2, half])
            share(t, i, 2)
    for t in (0, 1):
        own_local[t].wait()
        for i in range(4):
            for j in range(4):
                got(slot(t, i, j, core=1 - c), xd.at[t, i, j])
    aa_copy.wait()

    gu[...] = jnp.zeros_like(gu)
    rr[...] = jnp.zeros_like(rr)

    def forward(i, carry):
        for e in range(8, 16):
            @pl.when(i == e)
            def _():
                got(weights(wb, block_of(jnp.int32(e))), zr.at[e])
                if e <= 10 or e == 13:
                    zcopy(e, (e - 2) % 2, e + 4 if e <= 10 else 15).start()

        k = block_of(i)
        kx, ky, kc = lax.div(k, 4), lax.rem(lax.div(k, 2), 2) * 2, lax.rem(k, 2)
        t = jnp.concatenate([xb[0, kc, kx, ky], xb[0, kc, kx, ky + 1]], axis=1)
        u = jnp.concatenate([xb[1, kc, kx, ky], xb[1, kc, kx, ky + 1]], axis=1)
        gu[...] += tn(wb[k, :, 0:W + 2 * COLS], t)
        rr[...] += tn(wb[k, :, W + 2 * COLS:W + 3 * COLS], u)
        return carry

    lax.fori_loop(0, 16, forward, 0)

    @pl.when(home)
    def _():
        pltpu.make_async_copy(ab, ab, abs_.at[0]).wait()

    @pl.when(jnp.logical_not(home))
    def _():
        got(ab, abs_.at[0])

    low = gu[0:W].astype(BF16)
    b_t = ab[...].astype(F32).T.astype(BF16)
    step = 64
    ratio = jnp.zeros((1, 2 * ROWS), F32)
    for r in range(COLS // step):
        units = slice(r * step, (r + 1) * step)
        g_at, u_at = W + r * step, W + COLS + r * step
        gate, up, readout = gu[g_at:g_at + step], gu[u_at:u_at + step], rr[units]
        pol_gate = gate + adapter_scale * dot(b_t[units, 0:RANK], low[0:RANK])
        pol_up = up + adapter_scale * dot(b_t[units, RANK:W], low[RANK:W])
        sig = jax.nn.sigmoid(pol_gate)
        act = pol_gate * sig
        shift = act * pol_up - gate * jax.nn.sigmoid(gate) * up
        ratio += jnp.sum(shift * readout, axis=0, keepdims=True)
        scaled = readout * (1.0 / math.sqrt(D))
        hc[g_at:g_at + step] = (scaled * pol_up * (sig * (1.0 + pol_gate * (1.0 - sig)))).astype(BF16)
        hc[u_at:u_at + step] = (scaled * act).astype(BF16)
    lr_own[...] = ratio
    lrx[x, c] = ratio
    around = [(i, f) for i in range(4) for f in (0, 1) if i or f]

    def lr_send(i, f):
        n, core = 2 * i + f, 1 - c if f else c
        return copy(lr_own, lrx.at[x, c], lrs.at[n], lrr.at[n], dev(m4(x + i), y, z, core))

    def lr_send_y(i):
        return copy(lry.at[y], lry.at[y], lrs.at[7 + i], lrr.at[7 + i], dev(x, m4(y + i), z, c))

    for i, f in around:
        lr_send(i, f).start()
    hc[0:RANK] = (adapter_scale * dot(ab[0:RANK], hc[W:W + COLS])).astype(BF16)
    hc[RANK:W] = (adapter_scale * dot(ab[RANK:W], hc[W + COLS:])).astype(BF16)

    first, second = slice(0, CUT), slice(CUT, BLK)

    def order(j):
        turn = lax.rem(j + 1, 3)
        dx = jnp.where(j < 2, 2, jnp.where(turn == 0, 1, jnp.where(turn == 1, 3, 0)))
        dh = jnp.where(j < 2, 1 - j, jnp.where(j < 5, 1, 0))
        return lax.rem(x + dx, 4), lax.rem(yh + dh, 2)

    def product(j, core):
        bx, bh = order(j)
        return dot(wb[bx * 4 + bh * 2 + core, :, 0:W + 2 * COLS], hc[...])

    def to_sib(j):
        return copy(sb.at[j], rb.at[j], d2s.at[j], d2r.at[j], sib)

    def back_send(j):
        sb[j] = product(j, 1 - c).astype(BF16)
        to_sib(j).start()

    up_x, down_x = dev(m4(x + 1), y, z, c), dev(m4(x - 1), y, z, c)
    up_y, down_y = dev(x, m4(y + 1), z, c), dev(x, m4(y - 1), z, c)
    far, near = (1 - yh) * 2, yh * 2
    pairs = (pl.ds(far, 2), pl.ds(near, 2))

    def fold(idx, ref):
        pb[idx] = (pb[idx].astype(F32) + ref[...].astype(F32)).astype(BF16)

    def a1(d):
        return copy(pb.at[m4(x + 2), pairs[d], first], r1.at[d], ras.at[0, d], rar.at[0, d], (up_x, down_x)[d])

    def a2(d, n):
        return copy(
            pb.at[m4(x + 1 - 2 * d), pairs[n], first], r2.at[d, n], ras.at[1 + n, d], rar.at[1 + n, d], (up_x, down_x)[d]
        )

    def a_fold(d):
        got(r1.at[d], rar.at[0, d])
        fold((m4(x + 1 - 2 * d), pairs[d], first), r1.at[d])

    def b_dir(dx):
        return 0 if dx in (1, 2) else 1

    def b1(dx):
        d = b_dir(dx)
        return copy(pb.at[m4(x + dx), m4(y + 2), second], r3.at[dx], rbs.at[0, dx], rbr.at[0, dx], (up_y, down_y)[d])

    def b2(dx, d):
        return copy(
            pb.at[m4(x + dx), m4(y + 1 - 2 * d), second], r4.at[d, dx], rbs.at[1 + d, dx], rbr.at[1 + d, dx], (up_y, down_y)[d]
        )

    def b_fold(dx):
        got(r3.at[dx], rbr.at[0, dx])
        fold((m4(x + dx), m4(y + 1 - 2 * b_dir(dx)), second), r3.at[dx])

    def b_both(dx):
        b_fold(dx)
        b2(dx, 0).start()
        b2(dx, 1).start()

    def after(j):
        if j == 0:
            a1(0).start()
            b1(2).start()
        elif j == 1:
            a1(1).start()
        elif j == 2:
            b1(1).start()
        elif j == 3:
            b1(3).start()
            a2(1, 0).start()
        elif j == 4:
            b1(0).start()
            a_fold(0)
            a2(0, 0).start()
            b_both(2)
        elif j == 5:
            a2(0, 1).start()
            b_both(1)
        elif j == 6:
            a_fold(1)
            a2(1, 1).start()
            b_both(3)
        else:
            b_both(0)

    def az_send(i):
        return copy(apart.at[m8(z + i)], azb.at[z], azs.at[i], azr.at[i], dev(x, y, m8(z + i), c))

    def coefficients():
        for i in (1, 2, 3):
            got(lry.at[m4(y - i)], lrr.at[7 + i])
        lr_row = (((lry[0] + lry[1]) + lry[2]) + lry[3]) / math.sqrt(D)
        got(mb.at[1 - yl], mrs.at[1])
        eye2 = lax.broadcasted_iota(jnp.int32, (ROWS, ROWS), 0) == lax.broadcasted_iota(jnp.int32, (ROWS, ROWS), 1)

        def column(row):
            return jnp.sum(jnp.where(eye2, row, 0.0), axis=1, keepdims=True)

        for g in (0, 1):
            members = mb[g]
            pair = lax.shift_right_logical(members, 1)
            side = (1 - 2 * (members - 2 * pair)).astype(F32)
            pair = pair.astype(F32)
            lr_g = lr_row[:, g * ROWS:(g + 1) * ROWS]
            growth = jnp.exp(lr_g)
            same = column(pair) == pair
            margin = beta_coef * jnp.sum(jnp.where(same, column(side * (growth + lr_g)), 0.0), axis=0, keepdims=True)
            cf[g] = -loss_scale * beta_coef * jax.nn.sigmoid(-margin) * side * (growth + 1.0)

            @pl.when(yl == g)
            def _():
                lr_out[...] = lr_g

        low_t = (gu[0:W].astype(BF16).astype(F32) * jnp.concatenate([cf[0], cf[1]], axis=1)).astype(BF16)
        g_part = adapter_scale * nt(low_t[0:RANK], hc[W:W + COLS])
        u_part = adapter_scale * nt(low_t[RANK:W], hc[W + COLS:])
        apart[:, 0] = g_part.reshape(8, 8, COLS)
        apart[:, 1] = u_part.reshape(8, 8, COLS)
        for i in range(1, 8):
            az_send(i).start()
        azb[z] = apart[z]

    def a_near():
        return copy(afin.at[yl], abr.at[c], afs.at[0], afr.at[c], sib)

    def a_far():
        return copy(afin.at[1 - yl], abr.at[c], afs.at[1], afr.at[c], dev(x, other_y, z, yl))

    def hand_out():
        for i in range(1, 8):
            got(azb.at[m8(z - i)], azr.at[i])
        total = azb[0]
        for i in range(1, 8):
            total = total + azb[i]
        afin[...] = total

        a_far().start()

        @pl.when(home)
        def _():
            abr[c] = afin[yl]

        @pl.when(jnp.logical_not(home))
        def _():
            a_near().start()

    def log_ratios():
        for i, f in around:
            got(lrx.at[m4(x - i), 1 - c if f else c], lrr.at[2 * i + f])
        rows = [lrx[i, 0] + lrx[i, 1] for i in range(4)]
        lry[y] = ((rows[0] + rows[1]) + rows[2]) + rows[3]
        for i in (1, 2, 3):
            lr_send_y(i).start()

    back_send(0)

    def backward(j, carry):
        @pl.when(j < 7)
        def _():
            back_send(j + 1)

        total = product(j, c)
        to_sib(j).wait_recv()
        bx, bh = order(j)
        total = (total + rb[j].astype(F32)).astype(BF16)
        pb[bx, bh * 2] = total[:, 0:ROWS]
        pb[bx, bh * 2 + 1] = total[:, ROWS:]
        for e in range(8):
            @pl.when(j == e)
            def _():
                after(e)
                if e == 2:
                    log_ratios()
                if e == 6:
                    coefficients()
        return carry

    lax.fori_loop(0, 8, backward, 0)

    quarter = ((slice(0, 96), slice(96, CUT)), (slice(CUT, 256), slice(256, BLK)))
    size = ((96, CUT - 96), (256 - CUT, BLK - 256))
    span = (CUT, BLK - CUT)

    def near_of(h, i):
        return (x, m4(y + i)) if h == 0 else (m4(x + i), y)

    ways = ((up_y, down_y), (up_x, down_x))

    def c1(h, d):
        return copy(pb.at[near_of(h, 2) + (quarter[h][d],)], r5.at[h, d, 0:size[h][d]], rcs.at[0, h, d], rcr.at[0, h, d], ways[h][d])

    def c2(h, d):
        rows = (first, second)[h]
        return copy(pb.at[near_of(h, 1 - 2 * d) + (rows,)], r6.at[h, d, 0:span[h]], rcs.at[1, h, d], rcr.at[1, h, d], ways[h][d])

    def x_sum(n):
        for d in (0, 1):
            got(r2.at[d, n], rar.at[1 + n, d])
        idx = (x, pairs[n], first)
        pb[idx] = (pb[idx].astype(F32) + r2[0, n].astype(F32) + r2[1, n].astype(F32)).astype(BF16)

    def y_sum(i):
        for d in (0, 1):
            got(r4.at[d, i], rbr.at[1 + d, i])
        idx = (m4(x + i), y, second)
        pb[idx] = (pb[idx].astype(F32) + r4[0, i].astype(F32) + r4[1, i].astype(F32)).astype(BF16)

    def second_hop(h):
        for d in (0, 1):
            got(r5.at[h, d, 0:size[h][d]], rcr.at[0, h, d])
            fold(near_of(h, 1 - 2 * d) + (quarter[h][d],), r5.at[h, d, 0:size[h][d]])
            c2(h, d).start()

    x_sum(0)
    for d in (0, 1):
        c1(0, d).start()
    y_sum(2)
    for d in (0, 1):
        c1(1, d).start()
    x_sum(1)
    y_sum(1)
    second_hop(0)
    y_sum(3)
    second_hop(1)
    y_sum(0)
    hand_out()

    for h in (0, 1):
        for d in (0, 1):
            got(r6.at[h, d, 0:span[h]], rcr.at[1, h, d])
        rows = (first, second)[h]
        grad = pb[x, y, rows].astype(F32) + r6[h, 0, 0:span[h]].astype(F32) + r6[h, 1, 0:span[h]].astype(F32)
        ig_out[rows, :] = (grad * cf[yl]).astype(BF16)

    @pl.when(home)
    def _():
        got(abr.at[1 - c], afr.at[1 - c])

    @pl.when(jnp.logical_not(home))
    def _():
        got(abr.at[0], afr.at[0])
        got(abr.at[1], afr.at[1])

    abg_out[:, 0:COLS] = abr[0]
    abg_out[:, COLS:2 * COLS] = abr[1]

    for descriptor in pending:
        descriptor.wait_send()
    for e in (8, 9, 10, 13):
        zcopy(e, (e - 2) % 2, e + 4 if e <= 10 else 15).wait_send()

    def sent(j, carry):
        to_sib(j).wait_send()
        return carry

    lax.fori_loop(0, 8, sent, 0)
    for d in (0, 1):
        a1(d).wait_send()
        for n in (0, 1):
            a2(d, n).wait_send()
        for dx in range(4):
            b2(dx, d).wait_send()
        for h in (0, 1):
            c1(h, d).wait_send()
            c2(h, d).wait_send()
    for dx in range(4):
        b1(dx).wait_send()
    for i, f in around:
        lr_send(i, f).wait_send()
    for i in (1, 2, 3):
        lr_send_y(i).wait_send()
    for i in range(1, 8):
        az_send(i).wait_send()
    a_far().wait_send()

    @pl.when(jnp.logical_not(home))
    def _():
        a_near().wait_send()

    for b in (0, 1):
        @pl.when(home & (c != b))
        def _():
            for m in range(3):
                w0_near(b, m).wait_send()
            ab_near(b).wait_send()

        @pl.when(jnp.logical_not(home))
        def _():
            for m in range(3):
                w0_far(b, m).wait_send()


def hand_on(lr_in, ig_in, abg_in, lr_out, ig_out, abg_out):
    lr_out[...] = lr_in[0]
    ig_out[...] = ig_in[...]
    abg_out[...] = abg_in[...]


def on_device(tokens, upstream, gate_weight, up_weight, down_weight, adapter_a, adapter_b, membership):
    vmem, dma = pltpu.VMEM, pltpu.SemaphoreType.DMA
    anywhere = pl.BlockSpec(memory_space=pl.ANY)
    inside = pl.BlockSpec(memory_space=pltpu.VMEM)
    log_ratio, input_grad, b_gradient = pl.pallas_call(
        kernel,
        out_shape=(
            jax.ShapeDtypeStruct((1, ROWS), F32),
            jax.ShapeDtypeStruct((BLK, ROWS), BF16),
            jax.ShapeDtypeStruct((8, 2 * COLS), F32),
        ),
        in_specs=[anywhere] * 7 + [inside],
        out_specs=(inside,) * 3,
        scratch_shapes=[
            vmem((2, 2, 4, 4, BLK, ROWS), BF16),
            vmem((16, BLK, W + 3 * COLS), BF16),
            vmem((2 * RANK, COLS), BF16),
            vmem((2, 1, ROWS), jnp.int32),
            vmem((W + 2 * COLS, 2 * ROWS), F32),
            vmem((COLS, 2 * ROWS), F32),
            vmem((W + 2 * COLS, 2 * ROWS), BF16),
            vmem((8, BLK, 2 * ROWS), BF16),
            vmem((8, BLK, 2 * ROWS), BF16),
            vmem((4, 4, BLK, ROWS), BF16),
            vmem((2, 2, CUT, ROWS), BF16),
            vmem((2, 2, 2, CUT, ROWS), BF16),
            vmem((4, BLK - CUT, ROWS), BF16),
            vmem((2, 4, BLK - CUT, ROWS), BF16),
            vmem((2, 2, 96, ROWS), BF16),
            vmem((2, 2, CUT, ROWS), BF16),
            vmem((1, 2 * ROWS), F32),
            vmem((4, 2, 1, 2 * ROWS), F32),
            vmem((4, 1, 2 * ROWS), F32),
            vmem((2, 1, ROWS), F32),
            vmem((8, 2, 8, COLS), F32),
            vmem((8, 2, 8, COLS), F32),
            vmem((2, 8, COLS), F32),
            vmem((2, 8, COLS), F32),
            dma((2, 4, 4, 2)),
            dma((2, 4, 4)),
            dma((2, 24)),
            dma((2, 4, 4)),
            dma((2,)),
            dma((2, 3)),
            dma((2, 3)),
            dma((16,)),
            dma((2, 16)),
            dma((1,)),
            dma((2,)),
            dma((2,)),
            dma((8,)),
            dma((8,)),
            dma((3, 2)),
            dma((3, 2)),
            dma((3, 4)),
            dma((3, 4)),
            dma((2, 2, 2)),
            dma((2, 2, 2)),
            dma((11,)),
            dma((11,)),
            dma((8,)),
            dma((8,)),
            dma((2,)),
            dma((2,)),
        ],
        compiler_params=pltpu.CompilerParams(
            collective_id=0, has_side_effects=True, vmem_limit_bytes=56 * 1024 * 1024
        ),
    )(
        tokens.T, upstream.T, gate_weight, up_weight, down_weight,
        adapter_a.reshape(16, BLK, 2 * RANK), adapter_b, membership.reshape(1, ROWS),
    )
    log_ratio, input_grad, b_gradient = pl.pallas_call(
        hand_on,
        out_shape=(
            jax.ShapeDtypeStruct((ROWS,), F32),
            jax.ShapeDtypeStruct((BLK, ROWS), BF16),
            jax.ShapeDtypeStruct((8, 2 * COLS), F32),
        ),
        in_specs=[inside] * 3,
        out_specs=(inside,) * 3,
    )(log_ratio, input_grad, b_gradient)
    return log_ratio, input_grad.T, b_gradient


def solution(mesh):
    placed = (
        P("dp", "tensor"),
        P("dp", "tensor"),
        P("dp", "tensor"),
        P("dp", "tensor"),
        P("dp", "tensor"),
        P(),
        P(None, "tensor"),
        P("dp"),
    )
    return jax.shard_map(
        on_device,
        mesh=mesh,
        in_specs=placed,
        out_specs=(P("dp"), P("dp", "tensor"), P("dp", "tensor")),
        check_vma=False,
    )
```
